32 devices in a mesh: slab: 4 (over y, x), work: 8 (over z, core).
Axes of the slice: x: 2, y: 2, z: 4, core: 2. Of those that a mesh axis runs over, the one named last changes fastest.
Arguments:
- particles: float32 [8, 128, 128], P(None, ('slab', 'work')), may hold values from -5 to 5, as said below
- counts: int32 [128], P(('slab', 'work')), may hold values from 64 to 128
- partners: int32 [128, 8], P(('slab', 'work')), may hold values from 0 to 31
Outputs:
- density: float32 [128, 128], P(('slab', 'work'))
- acceleration: float32 [3, 128, 128], P(None, ('slab', 'work'))
The draws below stay inside these ranges and needn't reach their ends.
Inputs may be any that keep to these rules, and one draw needn't show every extreme that they name: `particles`: rows 0 to 2 hold positions in [0, 1], rows 3 to 5 velocities in [-5, 5], row 6 smoothing lengths in [0.6, 1.2], row 7 masses in [0.0005, 0.004]. Slots from counts[g] on are empty. `partners`: partner bins lie in the bin's own slab.
All inputs are finite; a program needn't handle non-finite values.
Results may differ from the reference program's by a relative error of at most 0.00005.
Values sent between devices are 32-bit elements; how exact they have to be, the bound alone decides.
A program may use at most 64 MiB of HBM per device.

```python
import jax
import jax.numpy as jnp
from jax import lax

P_SIZE = 128
K = 8
BINS_SLAB = 32
NBINS = 128
N_SLAB = 4


def draw_particles(key, part):
    subkeys = jax.random.split(key, 6)
    grid_shape = (NBINS, P_SIZE)
    places = jax.random.uniform(subkeys[1], (3, NBINS, P_SIZE), jnp.float32)
    speeds = jnp.clip(jax.random.normal(subkeys[3], (3, NBINS, P_SIZE), jnp.float32), -5.0, 5.0)
    lengths = jnp.exp(jax.random.uniform(subkeys[4], grid_shape, jnp.float32, jnp.log(0.6), jnp.log(1.2)))
    masses = jnp.exp(jax.random.uniform(subkeys[5], grid_shape, jnp.float32, jnp.log(0.0005), jnp.log(0.004)))
    return jnp.concatenate([places, speeds, lengths[None], masses[None]], axis=0).astype(jnp.float32)


def touch_ends(values, rng, least, largest):
    shape = values.shape
    index_at = [jax.random.randint(jax.random.fold_in(rng, axis), (), 0, shape[axis]) for axis in range(len(shape))]
    values = values.at[tuple(index_at)].set(least)
    longest = shape.index(max(shape))
    index_at[longest] = (index_at[longest] + 1) % shape[longest]
    return values.at[tuple(index_at)].set(largest)


def setup_inputs(seed: int = 0) -> dict:
    key_list = jax.random.split(jax.random.key(seed), 4)
    return {
        "particles": draw_particles(jax.random.fold_in(key_list[3], 71), 0),
        "counts": touch_ends(jax.random.randint(key_list[1], (NBINS,), P_SIZE // 2, P_SIZE + 1), jax.random.fold_in(key_list[1], 1), P_SIZE // 2, P_SIZE).astype(jnp.int32),
        "partners": touch_ends(jax.random.randint(key_list[2], (NBINS, K), 0, BINS_SLAB), jax.random.fold_in(key_list[2], 1), 0, BINS_SLAB - 1).astype(jnp.int32),
    }


weight_norm = 21.0 / (16.0 * 3.141592653589793)
force_norm = 105.0 / (16.0 * 3.141592653589793)
viscosity = 0.25

def separations(pos_self, pos_other):
    offset_vec = pos_self[:, :, None] - pos_other[:, None, :]
    radius = jnp.sqrt(lax.optimization_barrier(jnp.sum(offset_vec * offset_vec, axis=0)))
    return (offset_vec, radius)

def density_sum(pos_self, len_self, pos_other, mass_other):
    offset_vec, radius = separations(pos_self, pos_other)
    scaled = radius / len_self[:, None]
    shell_val = jnp.maximum(1.0 - 0.5 * scaled, 0.0)
    kernel = shell_val ** 4 * (1.0 + 2.0 * scaled) * (weight_norm / len_self ** 3)[:, None]
    return lax.optimization_barrier(jnp.sum(kernel * mass_other[None, :], axis=1))

def force_sum(pos_self, vel_self, len_self, rho_self, pos_other, vel_other, len_other, mass_other, rho_other):
    offset_vec, radius = separations(pos_self, pos_other)
    joint_h = 0.5 * (len_self[:, None] + len_other[None, :])
    scaled = radius / joint_h
    shell_val = jnp.maximum(1.0 - 0.5 * scaled, 0.0)
    factor = force_norm * shell_val ** 3 / joint_h ** 5 * mass_other[None, :]
    pressure = factor * (1.0 / rho_self[:, None] + 1.0 / rho_other[None, :])
    damping = factor * viscosity / (rho_self[:, None] * rho_other[None, :])
    veldiff = vel_self[:, :, None] - vel_other[:, None, :]
    return lax.optimization_barrier(jnp.sum(pressure[None] * offset_vec - damping[None] * veldiff, axis=2))

def reference(particles, counts, partners):
    slot_ids = jnp.arange(P_SIZE, dtype=jnp.int32)
    filled = (slot_ids[None, :] < counts[:, None]).astype(jnp.float32)
    masked = jnp.concatenate([particles[:7], particles[7:] * filled[None]], axis=0)
    bin_ids = jnp.arange(NBINS, dtype=jnp.int32)
    slab_ids = bin_ids // BINS_SLAB
    within = bin_ids % BINS_SLAB
    lower_bin = (slab_ids + N_SLAB - 1) % N_SLAB * BINS_SLAB + within
    upper_bin = (slab_ids + 1) % N_SLAB * BINS_SLAB + within
    linked = slab_ids[:, None] * BINS_SLAB + partners
    members = jnp.concatenate([bin_ids[:, None], lower_bin[:, None], upper_bin[:, None], linked], axis=1).astype(jnp.int32)

    def density_one(bin_index):
        gathered = jnp.take(masked, members[bin_index], axis=1).reshape(8, -1)
        own_bin = masked[:, bin_index]
        return density_sum(own_bin[0:3], own_bin[6], gathered[0:3], gathered[7])
    raw_density = lax.map(density_one, bin_ids)
    safe_density = filled * raw_density + (1.0 - filled)
    density = filled * raw_density
    full_state = jnp.concatenate([masked, safe_density[None]], axis=0)

    def force_one(bin_index):
        gathered = jnp.take(full_state, members[bin_index], axis=1).reshape(9, -1)
        own_bin = full_state[:, bin_index]
        result = force_sum(own_bin[0:3], own_bin[3:6], own_bin[6], own_bin[8], gathered[0:3], gathered[3:6], gathered[6], gathered[7], gathered[8])
        return result * filled[bin_index][None]
    acceleration = lax.map(force_one, bin_ids)
    return (density, jnp.transpose(acceleration, (1, 0, 2)))
```

```python
import functools

import jax
import jax.numpy as jnp
from jax import lax
from jax.experimental import pallas as pl
from jax.experimental.pallas import tpu as pltpu
from jax.sharding import PartitionSpec as P

weight_norm = 21.0 / (16.0 * 3.141592653589793)
force_norm = 105.0 / (16.0 * 3.141592653589793)
viscosity = 0.25

MESH = pl.DeviceIdType.MESH
F32 = jnp.float32
BF16 = jnp.bfloat16


def rounded(values):
    return values.astype(BF16).astype(F32)


def pieces(values):
    first = rounded(values)
    rest = values - first
    second = rounded(rest)
    return first, second, rest - second


def sub_iota(rows, slots):
    return lax.broadcasted_iota(jnp.int32, (rows, slots), 0)


def each(count, body):
    if count <= 16:
        for i in range(count):
            body(i)
    else:
        lax.fori_loop(0, count, lambda i, c: (body(i), c)[1], 0)


def kernel(
    n_slab,
    n_work,
    particles,
    counts,
    partners,
    density_out,
    accel_out,
    near,
    rest,
    invs,
    left_ops,
    h_wide,
    half_inv,
    right_ops,
    radius,
    force_hi,
    force_lo,
    sources,
    send_sem,
    recv_sem,
):
    nb, slots = particles.shape[1], particles.shape[2]
    links = partners.shape[1]
    members = 3 + links
    slab = lax.axis_index("slab")
    me = lax.axis_index("work")
    mine = me * nb
    slab_bins = n_work * nb
    up = lax.rem(slab + 1, n_slab)
    down = lax.rem(slab + n_slab - 1, n_slab)

    barrier = pltpu.get_barrier_semaphore()

    def greet(d):
        pl.semaphore_signal(
            barrier, 1, device_id={"work": lax.rem(me + d + 1, n_work)}, device_id_type=MESH
        )

    for other in (up, down):
        pl.semaphore_signal(barrier, 1, device_id={"slab": other}, device_id_type=MESH)
    each(n_work - 1, greet)

    lane = lax.broadcasted_iota(jnp.int32, (1, slots), 1)

    def filled_of(g):
        return (lane < counts[g]).astype(F32)

    for g in range(nb):
        state = particles[:, g, :]
        near[mine + g] = jnp.concatenate([state[0:3], state[7:8] * filled_of(g)], axis=0)
        rest[mine + g] = state[3:7]

    pl.semaphore_wait(barrier, n_work + 1)

    def send(buf, step):
        src = buf.at[pl.ds(mine, nb)]

        def start(dst, where):
            pltpu.make_async_remote_copy(
                src_ref=src,
                dst_ref=dst,
                send_sem=send_sem.at[step],
                recv_sem=recv_sem.at[step],
                device_id=where,
                device_id_type=MESH,
            ).start()

        each(n_work - 1, lambda d: start(src, {"work": lax.rem(me + d + 1, n_work)}))
        start(buf.at[pl.ds(slab_bins, nb)], {"slab": up})
        start(buf.at[pl.ds(slab_bins + nb, nb)], {"slab": down})

    def wait(buf, step, sem):
        block = buf.at[pl.ds(0, slab_bins + nb)]
        pltpu.make_async_copy(block, block, sem.at[step]).wait()

    send(near, 0)
    send(rest, 1)

    def member_index(g, k):
        if k == 0:
            return mine + g
        if k == 1:
            return slab_bins + g
        if k == 2:
            return slab_bins + nb + g
        return partners[g, k - 3]

    row4 = sub_iota(4, slots)
    row8 = sub_iota(8, slots)
    spare = jnp.zeros((8, slots), F32)

    def centre(g):
        return jnp.mean(particles[0:7, g, :], axis=1, keepdims=True)

    def offset(values, mid):
        shifted = jnp.where(row4 < 3, values - mid, 0.0)
        return shifted, jnp.sum(shifted * shifted, axis=0, keepdims=True)

    centres = []
    for g in range(nb):
        mid = centre(g)
        mid_pos = jnp.concatenate([mid[0:3], jnp.zeros((1, 1), F32)], axis=0)
        centres.append((mid_pos, mid[3:6]))
        shifted, length = offset(near[mine + g], mid_pos)
        own = jnp.where(row4 < 3, -2.0 * shifted, length)
        p0, p1, p2 = pieces(jnp.concatenate([own, own], axis=0))
        row = row8 % 4
        a0 = jnp.where(row < 3, p0, 1.0)
        left = jnp.concatenate(
            [
                a0,
                jnp.where(row8 < 4, a0, jnp.where(row < 3, p1, p0)),
                jnp.where(row8 < 4, p1, p2),
                spare,
            ],
            axis=0,
        )
        left_ops[g] = left.T.astype(BF16)
        h_row = particles[6, g : g + 1, :]
        h_wide[g] = jnp.broadcast_to(h_row, (slots, slots)).T
        half_inv[g] = jnp.broadcast_to(0.5 / h_row, (slots, slots)).T

    wait(near, 0, recv_sem)

    for g in range(nb):
        mid_pos, mid_vel = centres[g]
        for k in range(members):
            shifted, length = offset(near[member_index(g, k)], mid_pos)
            other = jnp.where(row4 < 3, shifted, length)
            q0, q1, q2 = pieces(jnp.concatenate([other, other], axis=0))
            row = row8 % 4
            one0 = jnp.where(row < 3, q0, 1.0)
            right = jnp.concatenate(
                [
                    jnp.where(row8 < 4, q0, q1),
                    jnp.where(row8 < 4, q2, one0),
                    jnp.where(row8 < 4, jnp.where(row < 3, q1, 1.0), one0),
                    spare,
                ],
                axis=0,
            )
            right_ops[g, :, k * slots : (k + 1) * slots] = right.astype(BF16)
        acc = jnp.zeros((slots, slots), F32)
        for k0 in range(0, members, 2):
            ks = range(k0, min(k0 + 2, members))
            square = jnp.dot(
                left_ops[g],
                right_ops[g, :, k0 * slots : (k0 + len(ks)) * slots],
                preferred_element_type=F32,
            )
            square = jnp.maximum(square, 1e-30)
            dist = square * lax.rsqrt(square)
            radius[g, :, k0 * slots : (k0 + len(ks)) * slots] = dist
            for k in ks:
                mass = near[member_index(g, k)][3:4]
                shell = jnp.maximum(
                    1.0 - dist[:, (k - k0) * slots : (k - k0 + 1) * slots] * half_inv[g], 0.0
                )
                shell2 = shell * shell
                acc += (shell2 * shell2) * ((1.25 - shell) * mass)
        total = jnp.sum(acc.T, axis=0, keepdims=True)
        filled = filled_of(g)
        h_row = particles[6, g : g + 1, :]
        raw = total * (4.0 * weight_norm / (h_row * h_row * h_row))
        density_out[g : g + 1, :] = filled * raw
        invs[mine + g] = 1.0 / (filled * raw + (1.0 - filled))

    send(invs, 2)
    wait(rest, 1, recv_sem)

    for g in range(nb):
        for k in range(members):
            cols = slice(k * slots, (k + 1) * slots)
            both = h_wide[g] + rest[member_index(g, k)][3:4]
            inv = 1.0 / both
            inv2 = inv * inv
            gap = jnp.maximum(both - radius[g, :, cols], 0.0)
            part = gap * inv2
            force = (part * part) * (part * inv2)
            high = force.astype(BF16)
            force_hi[g, :, cols] = high
            force_lo[g, :, cols] = (force - high.astype(F32)).astype(BF16)

    wait(invs, 2, recv_sem)

    for g in range(nb):
        mid_pos, mid_vel = centres[g]
        mid_four = jnp.concatenate([mid_vel, jnp.zeros((1, 1), F32)], axis=0)
        for k in range(members):
            at = member_index(g, k)
            place = near[at]
            mass = place[3:4]
            moment = jnp.where(row4 < 3, place - mid_pos, 1.0) * mass
            speed = (rest[at] - mid_four) * mass
            inv = invs[at]
            first = jnp.concatenate([moment, moment * inv], axis=0)
            second = jnp.where(row8 < 3, jnp.concatenate([speed, speed], axis=0) * inv, 0.0)
            b0, b1, b2 = pieces(jnp.concatenate([first, second], axis=0))
            sources[g, :, k * slots : (k + 1) * slots] = jnp.concatenate(
                [b0, b1, b2], axis=0
            ).astype(BF16)
        dims = (((1,), (1,)), ((), ()))
        sums = lax.dot_general(
            force_hi[g], sources[g], dims, preferred_element_type=F32
        ) + lax.dot_general(force_lo[g], sources[g], dims, preferred_element_type=F32)
        sums = sums.T
        sums = sums[0:16] + sums[16:32] + sums[32:48]
        own = particles[:, g, :]
        pos = own[0:3] - mid_pos[0:3]
        vel = own[3:6] - mid_vel
        inv = invs[mine + g]
        s1, s0, t1, t0, tv = sums[0:3], sums[3:4], sums[4:7], sums[7:8], sums[8:11]
        result = inv * (pos * s0 - s1) + (pos * t0 - t1) - (viscosity * inv) * (vel * t0 - tv)
        accel_out[:, g, :] = result * (filled_of(g) * (32.0 * force_norm))

    for step, buf in enumerate((near, rest, invs)):
        wait(buf, step, send_sem)


def per_device(n_slab, n_work, particles, counts, partners):
    channels, nb, slots = particles.shape
    members = 3 + partners.shape[1]
    bins = (n_work + 2) * nb
    vmem = pl.BlockSpec(memory_space=pltpu.VMEM)
    smem = pl.BlockSpec(memory_space=pltpu.SMEM)
    pairs = nb * members * slots * slots
    return pl.pallas_call(
        functools.partial(kernel, n_slab, n_work),
        out_shape=(
            jax.ShapeDtypeStruct((nb, slots), F32),
            jax.ShapeDtypeStruct((3, nb, slots), F32),
        ),
        in_specs=[vmem, smem, smem],
        out_specs=(vmem, vmem),
        scratch_shapes=[
            pltpu.VMEM((bins, 4, slots), F32),
            pltpu.VMEM((bins, 4, slots), F32),
            pltpu.VMEM((bins, 1, slots), F32),
            pltpu.VMEM((nb, slots, 32), BF16),
            pltpu.VMEM((nb, slots, slots), F32),
            pltpu.VMEM((nb, slots, slots), F32),
            pltpu.VMEM((nb, 32, members * slots), BF16),
            pltpu.VMEM((nb, slots, members * slots), F32),
            pltpu.VMEM((nb, slots, members * slots), BF16),
            pltpu.VMEM((nb, slots, members * slots), BF16),
            pltpu.VMEM((nb, 48, members * slots), BF16),
            pltpu.SemaphoreType.DMA((3,)),
            pltpu.SemaphoreType.DMA((3,)),
        ],
        compiler_params=pltpu.CompilerParams(
            collective_id=0, has_side_effects=True, vmem_limit_bytes=40 * 1024 * 1024
        ),
        cost_estimate=pl.CostEstimate(flops=40 * pairs, bytes_accessed=65536, transcendentals=0),
    )(particles, counts, partners)


def solution(mesh):
    placed = (P(None, ("slab", "work"), None), P(("slab", "work")), P(("slab", "work"), None))
    return jax.shard_map(
        functools.partial(per_device, mesh.shape["slab"], mesh.shape["work"]),
        mesh=mesh,
        in_specs=placed,
        out_specs=(P(("slab", "work"), None), P(None, ("slab", "work"), None)),
        check_vma=False,
    )
```

```python
import functools

import jax
import jax.numpy as jnp
from jax import lax
from jax.experimental import pallas as pl
from jax.experimental.pallas import tpu as pltpu
from jax.sharding import PartitionSpec as P

weight_norm = 21.0 / (16.0 * 3.141592653589793)
force_norm = 105.0 / (16.0 * 3.141592653589793)
viscosity = 0.25

MESH = pl.DeviceIdType.MESH
F32 = jnp.float32
BF16 = jnp.bfloat16


def rounded(values):
    return values.astype(BF16).astype(F32)


def pieces(values):
    first = rounded(values)
    rest = values - first
    second = rounded(rest)
    return first, second, rest - second


def sub_iota(rows, slots):
    return lax.broadcasted_iota(jnp.int32, (rows, slots), 0)


def each(count, body):
    if count <= 16:
        for i in range(count):
            body(i)
    else:
        lax.fori_loop(0, count, lambda i, c: (body(i), c)[1], 0)


def kernel(
    n_slab,
    n_work,
    particles_in,
    counts_in,
    partners_in,
    density_out,
    accel_out,
    particles,
    counts,
    partners,
    near,
    rest,
    invs,
    left_ops,
    h_wide,
    half_inv,
    right_ops,
    radius,
    force_hi,
    force_lo,
    sources,
    send_sem,
    recv_sem,
    read_sem,
):
    nb, slots = particles.shape[1], particles.shape[2]
    links = partners.shape[1]
    members = 3 + links
    slab = lax.axis_index("slab")
    me = lax.axis_index("work")
    mine = me * nb
    slab_bins = n_work * nb
    up = lax.rem(slab + 1, n_slab)
    down = lax.rem(slab + n_slab - 1, n_slab)

    reads = [
        pltpu.make_async_copy(src, dst, read_sem.at[i])
        for i, (src, dst) in enumerate(
            ((particles_in, particles), (counts_in, counts), (partners_in, partners))
        )
    ]
    for read in reads:
        read.start()

    barrier = pltpu.get_barrier_semaphore()

    def greet(d):
        pl.semaphore_signal(
            barrier, 1, device_id={"work": lax.rem(me + d + 1, n_work)}, device_id_type=MESH
        )

    for other in (up, down):
        pl.semaphore_signal(barrier, 1, device_id={"slab": other}, device_id_type=MESH)
    each(n_work - 1, greet)

    lane = lax.broadcasted_iota(jnp.int32, (1, slots), 1)

    def filled_of(g):
        return (lane < counts[g]).astype(F32)

    for read in reads:
        read.wait()
    for g in range(nb):
        state = particles[:, g, :]
        near[mine + g] = jnp.concatenate([state[0:3], state[7:8] * filled_of(g)], axis=0)
        rest[mine + g] = state[3:7]

    pl.semaphore_wait(barrier, n_work + 1)

    def send(buf, step):
        src = buf.at[pl.ds(mine, nb)]

        def start(dst, where):
            pltpu.make_async_remote_copy(
                src_ref=src,
                dst_ref=dst,
                send_sem=send_sem.at[step],
                recv_sem=recv_sem.at[step],
                device_id=where,
                device_id_type=MESH,
            ).start()

        each(n_work - 1, lambda d: start(src, {"work": lax.rem(me + d + 1, n_work)}))
        start(buf.at[pl.ds(slab_bins, nb)], {"slab": up})
        start(buf.at[pl.ds(slab_bins + nb, nb)], {"slab": down})

    def wait(buf, step, sem):
        block = buf.at[pl.ds(0, slab_bins + nb)]
        pltpu.make_async_copy(block, block, sem.at[step]).wait()

    send(near, 0)

    def member_index(g, k):
        if k == 0:
            return mine + g
        if k == 1:
            return slab_bins + g
        if k == 2:
            return slab_bins + nb + g
        return partners[g, k - 3]

    row4 = sub_iota(4, slots)
    row8 = sub_iota(8, slots)
    spare = jnp.zeros((8, slots), F32)

    def centre(g):
        return jnp.mean(particles[0:7, g, :], axis=1, keepdims=True)

    def offset(values, mid):
        shifted = jnp.where(row4 < 3, values - mid, 0.0)
        return shifted, jnp.sum(shifted * shifted, axis=0, keepdims=True)

    def build_right(g, k, mid_pos):
        shifted, length = offset(near[member_index(g, k)], mid_pos)
        other = jnp.where(row4 < 3, shifted, length)
        q0, q1, q2 = pieces(jnp.concatenate([other, other], axis=0))
        row = row8 % 4
        one0 = jnp.where(row < 3, q0, 1.0)
        right = jnp.concatenate(
            [
                jnp.where(row8 < 4, q0, q1),
                jnp.where(row8 < 4, q2, one0),
                jnp.where(row8 < 4, jnp.where(row < 3, q1, 1.0), one0),
                spare,
            ],
            axis=0,
        )
        right_ops[g, :, k * slots : (k + 1) * slots] = right.astype(BF16)

    centres = []
    for g in range(nb):
        mid = centre(g)
        mid_pos = jnp.concatenate([mid[0:3], jnp.zeros((1, 1), F32)], axis=0)
        centres.append((mid_pos, mid[3:6]))
        shifted, length = offset(near[mine + g], mid_pos)
        own = jnp.where(row4 < 3, -2.0 * shifted, length)
        p0, p1, p2 = pieces(jnp.concatenate([own, own], axis=0))
        row = row8 % 4
        a0 = jnp.where(row < 3, p0, 1.0)
        left = jnp.concatenate(
            [
                a0,
                jnp.where(row8 < 4, a0, jnp.where(row < 3, p1, p0)),
                jnp.where(row8 < 4, p1, p2),
                spare,
            ],
            axis=0,
        )
        left_ops[g] = left.T.astype(BF16)
        build_right(g, 0, mid_pos)
        h_row = particles[6, g : g + 1, :]
        h_wide[g] = jnp.broadcast_to(h_row, (slots, slots)).T
        half_inv[g] = jnp.broadcast_to(0.5 / h_row, (slots, slots)).T

    wait(near, 0, recv_sem)
    send(rest, 1)

    for g in range(nb):
        mid_pos, mid_vel = centres[g]
        for k in range(1, members):
            build_right(g, k, mid_pos)
        acc = jnp.zeros((slots, slots), F32)
        for k0 in range(0, members, 2):
            ks = range(k0, min(k0 + 2, members))
            square = jnp.dot(
                left_ops[g],
                right_ops[g, :, k0 * slots : (k0 + len(ks)) * slots],
                preferred_element_type=F32,
            )
            square = jnp.maximum(square, 1e-30)
            dist = square * lax.rsqrt(square)
            radius[g, :, k0 * slots : (k0 + len(ks)) * slots] = dist
            for k in ks:
                mass = near[member_index(g, k)][3:4]
                shell = jnp.maximum(
                    1.0 - dist[:, (k - k0) * slots : (k - k0 + 1) * slots] * half_inv[g], 0.0
                )
                shell2 = shell * shell
                acc += (shell2 * shell2) * ((1.25 - shell) * mass)
        total = jnp.sum(acc.T, axis=0, keepdims=True)
        filled = filled_of(g)
        h_row = particles[6, g : g + 1, :]
        raw = total * (4.0 * weight_norm / (h_row * h_row * h_row))
        density_out[g : g + 1, :] = filled * raw
        invs[mine + g] = 1.0 / (filled * raw + (1.0 - filled))

    send(invs, 2)
    wait(rest, 1, recv_sem)

    for g in range(nb):
        for k in range(members):
            cols = slice(k * slots, (k + 1) * slots)
            both = h_wide[g] + rest[member_index(g, k)][3:4]
            inv = pltpu.reciprocal(both, approx=True)
            inv2 = inv * inv
            gap = jnp.maximum(both - radius[g, :, cols], 0.0)
            part = gap * inv2
            force = (part * part) * (part * inv2)
            high = force.astype(BF16)
            force_hi[g, :, cols] = high
            force_lo[g, :, cols] = (force - high.astype(F32)).astype(BF16)

    wait(invs, 2, recv_sem)

    for g in range(nb):
        mid_pos, mid_vel = centres[g]
        mid_four = jnp.concatenate([mid_vel, jnp.zeros((1, 1), F32)], axis=0)
        for k in range(members):
            at = member_index(g, k)
            place = near[at]
            mass = place[3:4]
            moment = jnp.where(row4 < 3, place - mid_pos, 1.0) * mass
            speed = (rest[at] - mid_four) * mass
            inv = invs[at]
            first = jnp.concatenate([moment, moment * inv], axis=0)
            second = jnp.where(row8 < 3, jnp.concatenate([speed, speed], axis=0) * inv, 0.0)
            b0, b1, b2 = pieces(jnp.concatenate([first, second], axis=0))
            sources[g, :, k * slots : (k + 1) * slots] = jnp.concatenate(
                [b0, b1, b2], axis=0
            ).astype(BF16)
        dims = (((1,), (1,)), ((), ()))
        sums = lax.dot_general(
            force_hi[g], sources[g], dims, preferred_element_type=F32
        ) + lax.dot_general(force_lo[g], sources[g], dims, preferred_element_type=F32)
        sums = sums.T
        sums = sums[0:16] + sums[16:32] + sums[32:48]
        own = particles[:, g, :]
        pos = own[0:3] - mid_pos[0:3]
        vel = own[3:6] - mid_vel
        inv = invs[mine + g]
        s1, s0, t1, t0, tv = sums[0:3], sums[3:4], sums[4:7], sums[7:8], sums[8:11]
        result = inv * (pos * s0 - s1) + (pos * t0 - t1) - (viscosity * inv) * (vel * t0 - tv)
        accel_out[:, g, :] = result * (filled_of(g) * (32.0 * force_norm))

    for step, buf in enumerate((near, rest, invs)):
        wait(buf, step, send_sem)


def per_device(n_slab, n_work, particles, counts, partners):
    channels, nb, slots = particles.shape
    members = 3 + partners.shape[1]
    bins = (n_work + 2) * nb
    vmem = pl.BlockSpec(memory_space=pltpu.VMEM)
    hbm = pl.BlockSpec(memory_space=pltpu.HBM)
    pairs = nb * members * slots * slots
    return pl.pallas_call(
        functools.partial(kernel, n_slab, n_work),
        out_shape=(
            jax.ShapeDtypeStruct((nb, slots), F32),
            jax.ShapeDtypeStruct((3, nb, slots), F32),
        ),
        in_specs=[hbm, hbm, hbm],
        out_specs=(vmem, vmem),
        scratch_shapes=[
            pltpu.VMEM(particles.shape, F32),
            pltpu.SMEM(counts.shape, counts.dtype),
            pltpu.SMEM(partners.shape, partners.dtype),
            pltpu.VMEM((bins, 4, slots), F32),
            pltpu.VMEM((bins, 4, slots), F32),
            pltpu.VMEM((bins, 1, slots), F32),
            pltpu.VMEM((nb, slots, 32), BF16),
            pltpu.VMEM((nb, slots, slots), F32),
            pltpu.VMEM((nb, slots, slots), F32),
            pltpu.VMEM((nb, 32, members * slots), BF16),
            pltpu.VMEM((nb, slots, members * slots), F32),
            pltpu.VMEM((nb, slots, members * slots), BF16),
            pltpu.VMEM((nb, slots, members * slots), BF16),
            pltpu.VMEM((nb, 48, members * slots), BF16),
            pltpu.SemaphoreType.DMA((3,)),
            pltpu.SemaphoreType.DMA((3,)),
            pltpu.SemaphoreType.DMA((3,)),
        ],
        compiler_params=pltpu.CompilerParams(
            collective_id=0, has_side_effects=True, vmem_limit_bytes=64 * 1024 * 1024
        ),
        cost_estimate=pl.CostEstimate(flops=40 * pairs, bytes_accessed=65536, transcendentals=0),
    )(particles, counts, partners)


def solution(mesh):
    placed = (P(None, ("slab", "work"), None), P(("slab", "work")), P(("slab", "work"), None))
    return jax.shard_map(
        functools.partial(per_device, mesh.shape["slab"], mesh.shape["work"]),
        mesh=mesh,
        in_specs=placed,
        out_specs=(P(("slab", "work"), None), P(None, ("slab", "work"), None)),
        check_vma=False,
    )
```

```python
import functools

import jax
import jax.numpy as jnp
from jax import lax
from jax.experimental import pallas as pl
from jax.experimental.pallas import tpu as pltpu
from jax.sharding import PartitionSpec as P

weight_norm = 21.0 / (16.0 * 3.141592653589793)
force_norm = 105.0 / (16.0 * 3.141592653589793)
viscosity = 0.25

MESH = pl.DeviceIdType.MESH
F32 = jnp.float32
BF16 = jnp.bfloat16


def rounded(values):
    return values.astype(BF16).astype(F32)


def pieces(values):
    first = rounded(values)
    rest = values - first
    second = rounded(rest)
    return first, second, rest - second


def sub_iota(rows, slots):
    return lax.broadcasted_iota(jnp.int32, (rows, slots), 0)


def each(count, body):
    if count <= 16:
        for i in range(count):
            body(i)
    else:
        lax.fori_loop(0, count, lambda i, c: (body(i), c)[1], 0)


def kernel(
    n_slab,
    n_work,
    particles_in,
    counts_in,
    partners_in,
    density_out,
    accel_out,
    particles,
    counts,
    partners,
    near,
    rest,
    invs,
    left_ops,
    h_wide,
    reach,
    limit,
    right_ops,
    radius,
    force_hi,
    force_lo,
    sources,
    send_sem,
    recv_sem,
    read_sem,
):
    nb, slots = particles.shape[1], particles.shape[2]
    links = partners.shape[1]
    members = 3 + links
    slab = lax.axis_index("slab")
    me = lax.axis_index("work")
    mine = me * nb
    slab_bins = n_work * nb
    up = lax.rem(slab + 1, n_slab)
    down = lax.rem(slab + n_slab - 1, n_slab)

    reads = [
        pltpu.make_async_copy(src, dst, read_sem.at[i])
        for i, (src, dst) in enumerate(
            ((particles_in, particles), (counts_in, counts), (partners_in, partners))
        )
    ]
    for read in reads:
        read.start()

    barrier = pltpu.get_barrier_semaphore()

    def greet(d):
        pl.semaphore_signal(
            barrier, 1, device_id={"work": lax.rem(me + d + 1, n_work)}, device_id_type=MESH
        )

    for other in (up, down):
        pl.semaphore_signal(barrier, 1, device_id={"slab": other}, device_id_type=MESH)
    each(n_work - 1, greet)

    lane = lax.broadcasted_iota(jnp.int32, (1, slots), 1)

    def filled_of(g):
        return (lane < counts[g]).astype(F32)

    for read in reads:
        read.wait()
    for g in range(nb):
        state = particles[:, g, :]
        near[mine + g] = jnp.concatenate([state[0:3], state[7:8] * filled_of(g)], axis=0)
        rest[mine + g] = state[3:7]

    pl.semaphore_wait(barrier, n_work + 1)

    def send(buf, step):
        src = buf.at[pl.ds(mine, nb)]

        def start(dst, where):
            pltpu.make_async_remote_copy(
                src_ref=src,
                dst_ref=dst,
                send_sem=send_sem.at[step],
                recv_sem=recv_sem.at[step],
                device_id=where,
                device_id_type=MESH,
            ).start()

        each(n_work - 1, lambda d: start(src, {"work": lax.rem(me + d + 1, n_work)}))
        start(buf.at[pl.ds(slab_bins, nb)], {"slab": up})
        start(buf.at[pl.ds(slab_bins + nb, nb)], {"slab": down})

    def wait(buf, step, sem):
        block = buf.at[pl.ds(0, slab_bins + nb)]
        pltpu.make_async_copy(block, block, sem.at[step]).wait()

    send(near, 0)

    def member_index(g, k):
        if k == 0:
            return mine + g
        if k == 1:
            return slab_bins + g
        if k == 2:
            return slab_bins + nb + g
        return partners[g, k - 3]

    row4 = sub_iota(4, slots)
    row8 = sub_iota(8, slots)
    spare = jnp.zeros((8, slots), F32)

    def centre(g):
        return jnp.mean(particles[0:7, g, :], axis=1, keepdims=True)

    def offset(values, mid):
        shifted = jnp.where(row4 < 3, values - mid, 0.0)
        return shifted, jnp.sum(shifted * shifted, axis=0, keepdims=True)

    def build_right(g, k, mid_pos):
        shifted, length = offset(near[member_index(g, k)], mid_pos)
        other = jnp.where(row4 < 3, shifted, length)
        q0, q1, q2 = pieces(jnp.concatenate([other, other], axis=0))
        row = row8 % 4
        one0 = jnp.where(row < 3, q0, 1.0)
        right = jnp.concatenate(
            [
                jnp.where(row8 < 4, q0, q1),
                jnp.where(row8 < 4, q2, one0),
                jnp.where(row8 < 4, jnp.where(row < 3, q1, 1.0), one0),
                spare,
            ],
            axis=0,
        )
        right_ops[g, :, k * slots : (k + 1) * slots] = right.astype(BF16)

    centres = []
    for g in range(nb):
        mid = centre(g)
        mid_pos = jnp.concatenate([mid[0:3], jnp.zeros((1, 1), F32)], axis=0)
        centres.append((mid_pos, mid[3:6]))
        shifted, length = offset(near[mine + g], mid_pos)
        own = jnp.where(row4 < 3, -2.0 * shifted, length)
        p0, p1, p2 = pieces(jnp.concatenate([own, own], axis=0))
        row = row8 % 4
        a0 = jnp.where(row < 3, p0, 1.0)
        left = jnp.concatenate(
            [
                a0,
                jnp.where(row8 < 4, a0, jnp.where(row < 3, p1, p0)),
                jnp.where(row8 < 4, p1, p2),
                spare,
            ],
            axis=0,
        )
        left_ops[g] = left.T.astype(BF16)
        build_right(g, 0, mid_pos)
        h_row = particles[6, g : g + 1, :]
        h_wide[g] = jnp.broadcast_to(h_row, (slots, slots)).T
        reach[g] = 2.0 * h_wide[g]
        limit[g] = 2.5 * h_wide[g]

    wait(near, 0, recv_sem)
    send(rest, 1)

    for g in range(nb):
        mid_pos, mid_vel = centres[g]
        for k in range(1, members):
            build_right(g, k, mid_pos)
        acc = jnp.zeros((slots, slots), F32)
        for k0 in range(0, members, 2):
            ks = range(k0, min(k0 + 2, members))
            square = jnp.dot(
                left_ops[g],
                right_ops[g, :, k0 * slots : (k0 + len(ks)) * slots],
                preferred_element_type=F32,
            )
            square = jnp.maximum(square, 1e-30)
            dist = square * lax.rsqrt(square)
            radius[g, :, k0 * slots : (k0 + len(ks)) * slots] = dist
            for k in ks:
                mass = near[member_index(g, k)][3:4]
                gap = jnp.maximum(
                    reach[g] - dist[:, (k - k0) * slots : (k - k0 + 1) * slots], 0.0
                )
                gap2 = gap * gap
                acc += (gap2 * gap2) * ((limit[g] - gap) * mass)
        total = jnp.sum(acc.T, axis=0, keepdims=True)
        filled = filled_of(g)
        h_row = particles[6, g : g + 1, :]
        h2 = h_row * h_row
        raw = total * ((weight_norm / 8.0) / (h2 * h2 * h2 * h2))
        density_out[g : g + 1, :] = filled * raw
        invs[mine + g] = 1.0 / (filled * raw + (1.0 - filled))

    send(invs, 2)
    wait(rest, 1, recv_sem)

    for g in range(nb):
        for k in range(members):
            cols = slice(k * slots, (k + 1) * slots)
            both = h_wide[g] + rest[member_index(g, k)][3:4]
            inv = pltpu.reciprocal(both, approx=True)
            inv2 = inv * inv
            gap = jnp.maximum(both - radius[g, :, cols], 0.0)
            part = gap * inv2
            force = (part * part) * (part * inv2)
            high = force.astype(BF16)
            force_hi[g, :, cols] = high
            force_lo[g, :, cols] = (force - high.astype(F32)).astype(BF16)

    wait(invs, 2, recv_sem)

    for g in range(nb):
        mid_pos, mid_vel = centres[g]
        mid_four = jnp.concatenate([mid_vel, jnp.zeros((1, 1), F32)], axis=0)
        for k in range(members):
            at = member_index(g, k)
            place = near[at]
            mass = place[3:4]
            moment = jnp.where(row4 < 3, place - mid_pos, 1.0) * mass
            speed = (rest[at] - mid_four) * mass
            inv = invs[at]
            first = jnp.concatenate([moment, moment * inv], axis=0)
            second = jnp.where(row8 < 3, jnp.concatenate([speed, speed], axis=0) * inv, 0.0)
            b0, b1, b2 = pieces(jnp.concatenate([first, second], axis=0))
            sources[g, :, k * slots : (k + 1) * slots] = jnp.concatenate(
                [b0, b1, b2], axis=0
            ).astype(BF16)
        dims = (((1,), (1,)), ((), ()))
        sums = lax.dot_general(
            force_hi[g], sources[g], dims, preferred_element_type=F32
        ) + lax.dot_general(force_lo[g], sources[g], dims, preferred_element_type=F32)
        sums = sums.T
        sums = sums[0:16] + sums[16:32] + sums[32:48]
        own = particles[:, g, :]
        pos = own[0:3] - mid_pos[0:3]
        vel = own[3:6] - mid_vel
        inv = invs[mine + g]
        s1, s0, t1, t0, tv = sums[0:3], sums[3:4], sums[4:7], sums[7:8], sums[8:11]
        result = inv * (pos * s0 - s1) + (pos * t0 - t1) - (viscosity * inv) * (vel * t0 - tv)
        accel_out[:, g, :] = result * (filled_of(g) * (32.0 * force_norm))

    for step, buf in enumerate((near, rest, invs)):
        wait(buf, step, send_sem)


def per_device(n_slab, n_work, particles, counts, partners):
    channels, nb, slots = particles.shape
    members = 3 + partners.shape[1]
    bins = (n_work + 2) * nb
    vmem = pl.BlockSpec(memory_space=pltpu.VMEM)
    hbm = pl.BlockSpec(memory_space=pltpu.HBM)
    pairs = nb * members * slots * slots
    return pl.pallas_call(
        functools.partial(kernel, n_slab, n_work),
        out_shape=(
            jax.ShapeDtypeStruct((nb, slots), F32),
            jax.ShapeDtypeStruct((3, nb, slots), F32),
        ),
        in_specs=[hbm, hbm, hbm],
        out_specs=(vmem, vmem),
        scratch_shapes=[
            pltpu.VMEM(particles.shape, F32),
            pltpu.SMEM(counts.shape, counts.dtype),
            pltpu.SMEM(partners.shape, partners.dtype),
            pltpu.VMEM((bins, 4, slots), F32),
            pltpu.VMEM((bins, 4, slots), F32),
            pltpu.VMEM((bins, 1, slots), F32),
            pltpu.VMEM((nb, slots, 32), BF16),
            pltpu.VMEM((nb, slots, slots), F32),
            pltpu.VMEM((nb, slots, slots), F32),
            pltpu.VMEM((nb, slots, slots), F32),
            pltpu.VMEM((nb, 32, members * slots), BF16),
            pltpu.VMEM((nb, slots, members * slots), F32),
            pltpu.VMEM((nb, slots, members * slots), BF16),
            pltpu.VMEM((nb, slots, members * slots), BF16),
            pltpu.VMEM((nb, 48, members * slots), BF16),
            pltpu.SemaphoreType.DMA((3,)),
            pltpu.SemaphoreType.DMA((3,)),
            pltpu.SemaphoreType.DMA((3,)),
        ],
        compiler_params=pltpu.CompilerParams(
            collective_id=0, has_side_effects=True, vmem_limit_bytes=40 * 1024 * 1024
        ),
        cost_estimate=pl.CostEstimate(flops=40 * pairs, bytes_accessed=65536, transcendentals=0),
    )(*(pltpu.with_memory_space_constraint(a, pltpu.HBM) for a in (particles, counts, partners)))


def solution(mesh):
    placed = (P(None, ("slab", "work"), None), P(("slab", "work")), P(("slab", "work"), None))
    return jax.shard_map(
        functools.partial(per_device, mesh.shape["slab"], mesh.shape["work"]),
        mesh=mesh,
        in_specs=placed,
        out_specs=(P(("slab", "work"), None), P(None, ("slab", "work"), None)),
        check_vma=False,
    )
```

```python
import functools

import jax
import jax.numpy as jnp
from jax import lax
from jax.experimental import pallas as pl
from jax.experimental.pallas import tpu as pltpu
from jax.sharding import PartitionSpec as P

weight_norm = 21.0 / (16.0 * 3.141592653589793)
force_norm = 105.0 / (16.0 * 3.141592653589793)
viscosity = 0.25

MESH = pl.DeviceIdType.MESH
F32 = jnp.float32
BF16 = jnp.bfloat16


def rounded(values):
    return values.astype(BF16).astype(F32)


def pieces(values):
    first = rounded(values)
    rest = values - first
    second = rounded(rest)
    return first, second, rest - second


def sub_iota(rows, slots):
    return lax.broadcasted_iota(jnp.int32, (rows, slots), 0)


def each(count, body):
    if count <= 16:
        for i in range(count):
            body(i)
    else:
        lax.fori_loop(0, count, lambda i, c: (body(i), c)[1], 0)


def kernel(
    n_slab,
    n_work,
    particles_in,
    counts_in,
    partners_in,
    density_out,
    accel_out,
    particles,
    counts,
    partners,
    near,
    rest,
    invs,
    centres,
    left_ops,
    h_wide,
    reach,
    limit,
    right_ops,
    radius,
    force_hi,
    force_lo,
    sources,
    send_sem,
    recv_sem,
    read_sem,
):
    nb, slots = particles.shape[1], particles.shape[2]
    links = partners.shape[1]
    members = 3 + links
    slab = lax.axis_index("slab")
    me = lax.axis_index("work")
    mine = me * nb
    slab_bins = n_work * nb
    up = lax.rem(slab + 1, n_slab)
    down = lax.rem(slab + n_slab - 1, n_slab)

    reads = [
        pltpu.make_async_copy(src, dst, read_sem.at[i])
        for i, (src, dst) in enumerate(
            ((particles_in, particles), (counts_in, counts), (partners_in, partners))
        )
    ]
    for read in reads:
        read.start()

    barrier = pltpu.get_barrier_semaphore()

    def greet(d):
        pl.semaphore_signal(
            barrier, 1, device_id={"work": lax.rem(me + d + 1, n_work)}, device_id_type=MESH
        )

    for other in (up, down):
        pl.semaphore_signal(barrier, 1, device_id={"slab": other}, device_id_type=MESH)
    each(n_work - 1, greet)

    lane = lax.broadcasted_iota(jnp.int32, (1, slots), 1)

    def filled_of(g):
        return (lane < counts[g]).astype(F32)

    for read in reads:
        read.wait()
    for g in range(nb):
        state = particles[:, g, :]
        near[mine + g] = jnp.concatenate([state[0:3], state[7:8] * filled_of(g)], axis=0)
        rest[mine + g] = state[3:7]

    pl.semaphore_wait(barrier, n_work + 1)

    def send(buf, step):
        src = buf.at[pl.ds(mine, nb)]

        def start(dst, where):
            pltpu.make_async_remote_copy(
                src_ref=src,
                dst_ref=dst,
                send_sem=send_sem.at[step],
                recv_sem=recv_sem.at[step],
                device_id=where,
                device_id_type=MESH,
            ).start()

        each(n_work - 1, lambda d: start(src, {"work": lax.rem(me + d + 1, n_work)}))
        start(buf.at[pl.ds(slab_bins, nb)], {"slab": up})
        start(buf.at[pl.ds(slab_bins + nb, nb)], {"slab": down})

    def wait(buf, step, sem):
        block = buf.at[pl.ds(0, slab_bins + nb)]
        pltpu.make_async_copy(block, block, sem.at[step]).wait()

    send(near, 0)

    def member_index(g, k):
        if k == 0:
            return mine + g
        if k == 1:
            return slab_bins + g
        if k == 2:
            return slab_bins + nb + g
        return partners[g, k - 3]

    row4 = sub_iota(4, slots)
    row8 = sub_iota(8, slots)
    spare = jnp.zeros((8, slots), F32)

    def centre(g):
        return jnp.mean(particles[0:7, g, :], axis=1, keepdims=True)

    def offset(values, mid):
        shifted = jnp.where(row4 < 3, values - mid, 0.0)
        return shifted, jnp.sum(shifted * shifted, axis=0, keepdims=True)

    def build_right(g, k, mid_pos):
        shifted, length = offset(near[member_index(g, k)], mid_pos)
        other = jnp.where(row4 < 3, shifted, length)
        q0, q1, q2 = pieces(jnp.concatenate([other, other], axis=0))
        row = row8 % 4
        one0 = jnp.where(row < 3, q0, 1.0)
        right = jnp.concatenate(
            [
                jnp.where(row8 < 4, q0, q1),
                jnp.where(row8 < 4, q2, one0),
                jnp.where(row8 < 4, jnp.where(row < 3, q1, 1.0), one0),
                spare,
            ],
            axis=0,
        )
        right_ops[g, :, k * slots : (k + 1) * slots] = right.astype(BF16)

    def centres_of(g):
        mid = centres[g]
        return mid[0:4], mid[4:7]

    for g in range(nb):
        mid = centre(g)
        mid_pos = jnp.concatenate([mid[0:3], jnp.zeros((1, 1), F32)], axis=0)
        centres[g] = jnp.concatenate([mid_pos, mid[3:6], jnp.zeros((1, 1), F32)], axis=0)
        shifted, length = offset(near[mine + g], mid_pos)
        own = jnp.where(row4 < 3, -2.0 * shifted, length)
        p0, p1, p2 = pieces(jnp.concatenate([own, own], axis=0))
        row = row8 % 4
        a0 = jnp.where(row < 3, p0, 1.0)
        left = jnp.concatenate(
            [
                a0,
                jnp.where(row8 < 4, a0, jnp.where(row < 3, p1, p0)),
                jnp.where(row8 < 4, p1, p2),
                spare,
            ],
            axis=0,
        )
        left_ops[g] = left.T.astype(BF16)
        build_right(g, 0, mid_pos)
        h_row = particles[6, pl.ds(g, 1), :]
        h_wide[g] = jnp.broadcast_to(h_row, (slots, slots)).T
        reach[g] = 2.0 * h_wide[g]
        limit[g] = 2.5 * h_wide[g]

    wait(near, 0, recv_sem)
    send(rest, 1)

    @pl.loop(0, nb)
    def density_pass(g):
        mid_pos, mid_vel = centres_of(g)
        for k in range(1, members):
            build_right(g, k, mid_pos)
        acc = jnp.zeros((slots, slots), F32)
        for k0 in range(0, members, 2):
            ks = range(k0, min(k0 + 2, members))
            square = jnp.dot(
                left_ops[g],
                right_ops[g, :, k0 * slots : (k0 + len(ks)) * slots],
                preferred_element_type=F32,
            )
            square = jnp.maximum(square, 1e-30)
            dist = square * lax.rsqrt(square)
            radius[g, :, k0 * slots : (k0 + len(ks)) * slots] = dist
            for k in ks:
                mass = near[member_index(g, k)][3:4]
                gap = jnp.maximum(
                    reach[g] - dist[:, (k - k0) * slots : (k - k0 + 1) * slots], 0.0
                )
                gap2 = gap * gap
                acc += (gap2 * gap2) * ((limit[g] - gap) * mass)
        total = jnp.sum(acc.T, axis=0, keepdims=True)
        filled = filled_of(g)
        h_row = particles[6, pl.ds(g, 1), :]
        h2 = h_row * h_row
        raw = total * ((weight_norm / 8.0) / (h2 * h2 * h2 * h2))
        density_out[pl.ds(g, 1), :] = filled * raw
        invs[mine + g] = 1.0 / (filled * raw + (1.0 - filled))

    send(invs, 2)
    wait(rest, 1, recv_sem)

    @pl.loop(0, nb)
    def force_pass(g):
        for k in range(members):
            cols = slice(k * slots, (k + 1) * slots)
            both = h_wide[g] + rest[member_index(g, k)][3:4]
            inv = pltpu.reciprocal(both, approx=True)
            inv2 = inv * inv
            gap = jnp.maximum(both - radius[g, :, cols], 0.0)
            part = gap * inv2
            force = (part * part) * (part * inv2)
            high = force.astype(BF16)
            force_hi[g, :, cols] = high
            force_lo[g, :, cols] = (force - high.astype(F32)).astype(BF16)

    wait(invs, 2, recv_sem)

    @pl.loop(0, nb)
    def sum_pass(g):
        mid_pos, mid_vel = centres_of(g)
        mid_four = jnp.concatenate([mid_vel, jnp.zeros((1, 1), F32)], axis=0)
        for k in range(members):
            at = member_index(g, k)
            place = near[at]
            mass = place[3:4]
            moment = jnp.where(row4 < 3, place - mid_pos, 1.0) * mass
            speed = (rest[at] - mid_four) * mass
            inv = invs[at]
            first = jnp.concatenate([moment, moment * inv], axis=0)
            second = jnp.where(row8 < 3, jnp.concatenate([speed, speed], axis=0) * inv, 0.0)
            b0, b1, b2 = pieces(jnp.concatenate([first, second], axis=0))
            sources[g, :, k * slots : (k + 1) * slots] = jnp.concatenate(
                [b0, b1, b2], axis=0
            ).astype(BF16)
        dims = (((1,), (1,)), ((), ()))
        sums = lax.dot_general(
            force_hi[g], sources[g], dims, preferred_element_type=F32
        ) + lax.dot_general(force_lo[g], sources[g], dims, preferred_element_type=F32)
        sums = sums.T
        sums = sums[0:16] + sums[16:32] + sums[32:48]
        own = particles[:, g, :]
        pos = own[0:3] - mid_pos[0:3]
        vel = own[3:6] - mid_vel
        inv = invs[mine + g]
        s1, s0, t1, t0, tv = sums[0:3], sums[3:4], sums[4:7], sums[7:8], sums[8:11]
        result = inv * (pos * s0 - s1) + (pos * t0 - t1) - (viscosity * inv) * (vel * t0 - tv)
        accel_out[:, g, :] = result * (filled_of(g) * (32.0 * force_norm))

    for step, buf in enumerate((near, rest, invs)):
        wait(buf, step, send_sem)


def per_device(n_slab, n_work, particles, counts, partners):
    channels, nb, slots = particles.shape
    members = 3 + partners.shape[1]
    bins = (n_work + 2) * nb
    vmem = pl.BlockSpec(memory_space=pltpu.VMEM)
    hbm = pl.BlockSpec(memory_space=pltpu.HBM)
    pairs = nb * members * slots * slots
    return pl.pallas_call(
        functools.partial(kernel, n_slab, n_work),
        out_shape=(
            jax.ShapeDtypeStruct((nb, slots), F32),
            jax.ShapeDtypeStruct((3, nb, slots), F32),
        ),
        in_specs=[hbm, hbm, hbm],
        out_specs=(vmem, vmem),
        scratch_shapes=[
            pltpu.VMEM(particles.shape, F32),
            pltpu.SMEM(counts.shape, counts.dtype),
            pltpu.SMEM(partners.shape, partners.dtype),
            pltpu.VMEM((bins, 4, slots), F32),
            pltpu.VMEM((bins, 4, slots), F32),
            pltpu.VMEM((bins, 1, slots), F32),
            pltpu.VMEM((nb, 8, 1), F32),
            pltpu.VMEM((nb, slots, 32), BF16),
            pltpu.VMEM((nb, slots, slots), F32),
            pltpu.VMEM((nb, slots, slots), F32),
            pltpu.VMEM((nb, slots, slots), F32),
            pltpu.VMEM((nb, 32, members * slots), BF16),
            pltpu.VMEM((nb, slots, members * slots), F32),
            pltpu.VMEM((nb, slots, members * slots), BF16),
            pltpu.VMEM((nb, slots, members * slots), BF16),
            pltpu.VMEM((nb, 48, members * slots), BF16),
            pltpu.SemaphoreType.DMA((3,)),
            pltpu.SemaphoreType.DMA((3,)),
            pltpu.SemaphoreType.DMA((3,)),
        ],
        compiler_params=pltpu.CompilerParams(
            collective_id=0, has_side_effects=True, vmem_limit_bytes=40 * 1024 * 1024
        ),
        cost_estimate=pl.CostEstimate(flops=40 * pairs, bytes_accessed=65536, transcendentals=0),
    )(*(pltpu.with_memory_space_constraint(a, pltpu.HBM) for a in (particles, counts, partners)))


def solution(mesh):
    placed = (P(None, ("slab", "work"), None), P(("slab", "work")), P(("slab", "work"), None))
    return jax.shard_map(
        functools.partial(per_device, mesh.shape["slab"], mesh.shape["work"]),
        mesh=mesh,
        in_specs=placed,
        out_specs=(P(("slab", "work"), None), P(None, ("slab", "work"), None)),
        check_vma=False,
    )
```

```python
import functools

import jax
import jax.numpy as jnp
from jax import lax
from jax.experimental import pallas as pl
from jax.experimental.pallas import tpu as pltpu
from jax.sharding import PartitionSpec as P

weight_norm = 21.0 / (16.0 * 3.141592653589793)
force_norm = 105.0 / (16.0 * 3.141592653589793)
viscosity = 0.25

MESH = pl.DeviceIdType.MESH
F32 = jnp.float32
BF16 = jnp.bfloat16


def rounded(values):
    return values.astype(BF16).astype(F32)


def pieces(values):
    first = rounded(values)
    rest = values - first
    second = rounded(rest)
    return first, second, rest - second


def sub_iota(rows, slots):
    return lax.broadcasted_iota(jnp.int32, (rows, slots), 0)


def each(count, body):
    if count <= 16:
        for i in range(count):
            body(i)
    else:
        lax.fori_loop(0, count, lambda i, c: (body(i), c)[1], 0)


def kernel(
    n_slab,
    n_work,
    particles_in,
    counts_in,
    partners_in,
    density_out,
    accel_out,
    particles,
    counts,
    partners,
    near,
    rest,
    invs,
    left_ops,
    h_wide,
    reach,
    limit,
    right_ops,
    radius,
    force_hi,
    force_lo,
    partial,
    bases,
    sources,
    send_sem,
    recv_sem,
    read_sem,
):
    nb, slots = particles.shape[1], particles.shape[2]
    links = partners.shape[1]
    members = 3 + links
    slab = lax.axis_index("slab")
    me = lax.axis_index("work")
    mine = me * nb
    slab_bins = n_work * nb
    up = lax.rem(slab + 1, n_slab)
    down = lax.rem(slab + n_slab - 1, n_slab)

    reads = [
        pltpu.make_async_copy(src, dst, read_sem.at[i])
        for i, (src, dst) in enumerate(
            ((particles_in, particles), (counts_in, counts), (partners_in, partners))
        )
    ]
    for read in reads:
        read.start()

    barrier = pltpu.get_barrier_semaphore()

    def peer(d):
        if n_work & (n_work - 1):
            return lax.rem(me + d + 1, n_work)
        flips, other, bit = n_work - 1 - d, me, 1
        while bit < n_work:
            other = other + bit * ((flips // bit) % 2) * (1 - 2 * ((me // bit) % 2))
            bit *= 2
        return other

    def greet(d):
        pl.semaphore_signal(barrier, 1, device_id={"work": peer(d)}, device_id_type=MESH)

    each(n_work - 1, greet)
    for other in (up, down):
        pl.semaphore_signal(barrier, 1, device_id={"slab": other}, device_id_type=MESH)

    lane = lax.broadcasted_iota(jnp.int32, (1, slots), 1)

    def filled_of(g):
        return (lane < counts[g]).astype(F32)

    for read in reads:
        read.wait()
    for g in range(nb):
        state = particles[:, g, :]
        near[mine + g] = jnp.concatenate([state[0:3], state[7:8] * filled_of(g)], axis=0)
        rest[mine + g] = state[3:7]

    pl.semaphore_wait(barrier, n_work + 1)

    def send(buf, step, slab_step):
        src = buf.at[pl.ds(mine, nb)]

        def start(dst, where, arrived):
            pltpu.make_async_remote_copy(
                src_ref=src,
                dst_ref=dst,
                send_sem=send_sem.at[step],
                recv_sem=recv_sem.at[arrived],
                device_id=where,
                device_id_type=MESH,
            ).start()

        start(buf.at[pl.ds(slab_bins, nb)], {"slab": up}, slab_step)
        start(buf.at[pl.ds(slab_bins + nb, nb)], {"slab": down}, slab_step)
        each(n_work - 1, lambda d: start(src, {"work": peer(d)}, step))

    def wait(buf, bins, sem):
        block = buf.at[pl.ds(0, bins)]
        pltpu.make_async_copy(block, block, sem).wait()

    everyone = slab_bins + nb
    send(near, 0, 3)

    def member_index(g, k):
        if k == 0:
            return mine + g
        if k == 1:
            return slab_bins + g
        if k == 2:
            return slab_bins + nb + g
        return partners[g, k - 3]

    row4 = sub_iota(4, slots)
    row8 = sub_iota(8, slots)
    spare = jnp.zeros((8, slots), F32)

    def centre(g):
        return jnp.mean(particles[0:7, g, :], axis=1, keepdims=True)

    def offset(values, mid):
        shifted = jnp.where(row4 < 3, values - mid, 0.0)
        return shifted, jnp.sum(shifted * shifted, axis=0, keepdims=True)

    def build_right(g, k, mid_pos):
        shifted, length = offset(near[member_index(g, k)], mid_pos)
        other = jnp.where(row4 < 3, shifted, length)
        q0, q1, q2 = pieces(jnp.concatenate([other, other], axis=0))
        row = row8 % 4
        one0 = jnp.where(row < 3, q0, 1.0)
        right = jnp.concatenate(
            [
                jnp.where(row8 < 4, q0, q1),
                jnp.where(row8 < 4, q2, one0),
                jnp.where(row8 < 4, jnp.where(row < 3, q1, 1.0), one0),
                spare,
            ],
            axis=0,
        )
        right_ops[g, :, k * slots : (k + 1) * slots] = right.astype(BF16)

    centres = []
    for g in range(nb):
        mid = centre(g)
        mid_pos = jnp.concatenate([mid[0:3], jnp.zeros((1, 1), F32)], axis=0)
        centres.append((mid_pos, mid[3:6]))
        shifted, length = offset(near[mine + g], mid_pos)
        own = jnp.where(row4 < 3, -2.0 * shifted, length)
        p0, p1, p2 = pieces(jnp.concatenate([own, own], axis=0))
        row = row8 % 4
        a0 = jnp.where(row < 3, p0, 1.0)
        left = jnp.concatenate(
            [
                a0,
                jnp.where(row8 < 4, a0, jnp.where(row < 3, p1, p0)),
                jnp.where(row8 < 4, p1, p2),
                spare,
            ],
            axis=0,
        )
        left_ops[g] = left.T.astype(BF16)
        build_right(g, 0, mid_pos)
        h_row = particles[6, g : g + 1, :]
        h_wide[g] = jnp.broadcast_to(h_row, (slots, slots)).T
        reach[g] = 2.0 * h_wide[g]
        limit[g] = 2.5 * h_wide[g]

    def density_part(g, ks, acc):
        mid_pos = centres[g][0]
        for k in ks:
            if k:
                build_right(g, k, mid_pos)
        for k0 in range(ks[0], ks[-1] + 1, 2):
            pair = [k for k in (k0, k0 + 1) if k in ks]
            cols = slice(k0 * slots, (k0 + len(pair)) * slots)
            square = jnp.dot(left_ops[g], right_ops[g, :, cols], preferred_element_type=F32)
            square = jnp.maximum(square, 1e-30)
            dist = square * lax.rsqrt(square)
            radius[g, :, cols] = dist
            for k in pair:
                mass = near[member_index(g, k)][3:4]
                gap = jnp.maximum(
                    reach[g] - dist[:, (k - k0) * slots : (k - k0 + 1) * slots], 0.0
                )
                gap2 = gap * gap
                acc += (gap2 * gap2) * ((limit[g] - gap) * mass)
        return acc

    wait(near, 2 * nb, recv_sem.at[3])
    for g in range(nb):
        partial[g] = density_part(g, range(3), jnp.zeros((slots, slots), F32))
    wait(near, slab_bins - nb, recv_sem.at[0])
    send(rest, 1, 1)

    for g in range(nb):
        acc = density_part(g, range(3, members), partial[g])
        total = jnp.sum(acc.T, axis=0, keepdims=True)
        filled = filled_of(g)
        h_row = particles[6, g : g + 1, :]
        h2 = h_row * h_row
        raw = total * ((weight_norm / 8.0) / (h2 * h2 * h2 * h2))
        density_out[g : g + 1, :] = filled * raw
        invs[mine + g] = 1.0 / (filled * raw + (1.0 - filled))

    send(invs, 2, 2)
    wait(rest, everyone, recv_sem.at[1])

    for g in range(nb):
        for k in range(members):
            cols = slice(k * slots, (k + 1) * slots)
            both = h_wide[g] + rest[member_index(g, k)][3:4]
            inv = pltpu.reciprocal(both, approx=True)
            inv2 = inv * inv
            gap = jnp.maximum(both - radius[g, :, cols], 0.0)
            part = gap * inv2
            force = (part * part) * (part * inv2)
            high = force.astype(BF16)
            force_hi[g, :, cols] = high
            force_lo[g, :, cols] = (force - high.astype(F32)).astype(BF16)

    for g in range(nb):
        mid_pos, mid_vel = centres[g]
        mid_four = jnp.concatenate([mid_vel, jnp.zeros((1, 1), F32)], axis=0)
        for k in range(members):
            at = member_index(g, k)
            place = near[at]
            mass = place[3:4]
            moment = jnp.where(row4 < 3, place - mid_pos, 1.0) * mass
            speed = jnp.where(row4 < 3, rest[at] - mid_four, 0.0) * mass
            cols = slice(k * slots, (k + 1) * slots)
            bases[g, 0:8, cols] = jnp.concatenate([moment, moment], axis=0)
            bases[g, 8:16, cols] = jnp.concatenate([speed, speed], axis=0)

    wait(invs, everyone, recv_sem.at[2])

    for g in range(nb):
        mid_pos, mid_vel = centres[g]
        for k in range(members):
            cols = slice(k * slots, (k + 1) * slots)
            inv = invs[member_index(g, k)]
            source = jnp.concatenate(
                [
                    bases[g, 0:8, cols] * jnp.where(row8 < 4, 1.0, inv),
                    bases[g, 8:16, cols] * inv,
                ],
                axis=0,
            )
            first = source.astype(BF16)
            sources[g, 0:16, cols] = first
            sources[g, 16:32, cols] = (source - first.astype(F32)).astype(BF16)
        dims = (((1,), (1,)), ((), ()))
        sums = lax.dot_general(
            force_hi[g], sources[g], dims, preferred_element_type=F32
        ) + lax.dot_general(force_lo[g], sources[g], dims, preferred_element_type=F32)
        sums = sums.T
        sums = sums[0:16] + sums[16:32]
        own = particles[:, g, :]
        pos = own[0:3] - mid_pos[0:3]
        vel = own[3:6] - mid_vel
        inv = invs[mine + g]
        s1, s0, t1, t0, tv = sums[0:3], sums[3:4], sums[4:7], sums[7:8], sums[8:11]
        result = inv * (pos * s0 - s1) + (pos * t0 - t1) - (viscosity * inv) * (vel * t0 - tv)
        accel_out[:, g, :] = result * (filled_of(g) * (32.0 * force_norm))

    for step, buf in enumerate((near, rest, invs)):
        wait(buf, everyone, send_sem.at[step])


def per_device(n_slab, n_work, particles, counts, partners):
    channels, nb, slots = particles.shape
    members = 3 + partners.shape[1]
    bins = (n_work + 2) * nb
    vmem = pl.BlockSpec(memory_space=pltpu.VMEM)
    hbm = pl.BlockSpec(memory_space=pltpu.HBM)
    pairs = nb * members * slots * slots
    return pl.pallas_call(
        functools.partial(kernel, n_slab, n_work),
        out_shape=(
            jax.ShapeDtypeStruct((nb, slots), F32),
            jax.ShapeDtypeStruct((3, nb, slots), F32),
        ),
        in_specs=[hbm, hbm, hbm],
        out_specs=(vmem, vmem),
        scratch_shapes=[
            pltpu.VMEM(particles.shape, F32),
            pltpu.SMEM(counts.shape, counts.dtype),
            pltpu.SMEM(partners.shape, partners.dtype),
            pltpu.VMEM((bins, 4, slots), F32),
            pltpu.VMEM((bins, 4, slots), F32),
            pltpu.VMEM((bins, 1, slots), F32),
            pltpu.VMEM((nb, slots, 32), BF16),
            pltpu.VMEM((nb, slots, slots), F32),
            pltpu.VMEM((nb, slots, slots), F32),
            pltpu.VMEM((nb, slots, slots), F32),
            pltpu.VMEM((nb, 32, members * slots), BF16),
            pltpu.VMEM((nb, slots, members * slots), F32),
            pltpu.VMEM((nb, slots, members * slots), BF16),
            pltpu.VMEM((nb, slots, members * slots), BF16),
            pltpu.VMEM((nb, slots, slots), F32),
            pltpu.VMEM((nb, 16, members * slots), F32),
            pltpu.VMEM((nb, 32, members * slots), BF16),
            pltpu.SemaphoreType.DMA((3,)),
            pltpu.SemaphoreType.DMA((4,)),
            pltpu.SemaphoreType.DMA((3,)),
        ],
        compiler_params=pltpu.CompilerParams(
            collective_id=0, has_side_effects=True, vmem_limit_bytes=40 * 1024 * 1024
        ),
        cost_estimate=pl.CostEstimate(flops=40 * pairs, bytes_accessed=65536, transcendentals=0),
    )(*(pltpu.with_memory_space_constraint(a, pltpu.HBM) for a in (particles, counts, partners)))


def solution(mesh):
    placed = (P(None, ("slab", "work"), None), P(("slab", "work")), P(("slab", "work"), None))
    return jax.shard_map(
        functools.partial(per_device, mesh.shape["slab"], mesh.shape["work"]),
        mesh=mesh,
        in_specs=placed,
        out_specs=(P(("slab", "work"), None), P(None, ("slab", "work"), None)),
        check_vma=False,
    )
```

```python
import functools

import jax
import jax.numpy as jnp
from jax import lax
from jax.experimental import pallas as pl
from jax.experimental.pallas import tpu as pltpu
from jax.sharding import PartitionSpec as P

weight_norm = 21.0 / (16.0 * 3.141592653589793)
force_norm = 105.0 / (16.0 * 3.141592653589793)
viscosity = 0.25

MESH = pl.DeviceIdType.MESH
F32 = jnp.float32
BF16 = jnp.bfloat16


def rounded(values):
    return values.astype(BF16).astype(F32)


def pieces(values):
    first = rounded(values)
    rest = values - first
    second = rounded(rest)
    return first, second, rest - second


def sub_iota(rows, slots):
    return lax.broadcasted_iota(jnp.int32, (rows, slots), 0)


def each(count, body):
    if count <= 16:
        for i in range(count):
            body(i)
    else:
        lax.fori_loop(0, count, lambda i, c: (body(i), c)[1], 0)


def kernel(
    n_slab,
    n_work,
    particles_in,
    counts_in,
    partners_in,
    density_out,
    accel_out,
    particles,
    counts,
    partners,
    near,
    rest,
    invs,
    left_ops,
    h_wide,
    reach,
    limit,
    right_ops,
    radius,
    force_hi,
    force_lo,
    partial,
    bases,
    sources,
    send_sem,
    recv_sem,
    read_sem,
):
    nb, slots = particles.shape[1], particles.shape[2]
    links = partners.shape[1]
    members = 3 + links
    slab = lax.axis_index("slab")
    me = lax.axis_index("work")
    mine = me * nb
    slab_bins = n_work * nb
    up = lax.rem(slab + 1, n_slab)
    down = lax.rem(slab + n_slab - 1, n_slab)

    reads = [
        pltpu.make_async_copy(src, dst, read_sem.at[i])
        for i, (src, dst) in enumerate(
            ((particles_in, particles), (counts_in, counts), (partners_in, partners))
        )
    ]
    for read in reads:
        read.start()

    barrier = pltpu.get_barrier_semaphore()

    def peer(d):
        if n_work & (n_work - 1):
            return lax.rem(me + d + 1, n_work)
        flips, other, bit = n_work - 1 - d, me, 1
        while bit < n_work:
            other = other + bit * ((flips // bit) % 2) * (1 - 2 * ((me // bit) % 2))
            bit *= 2
        return other

    def greet(d):
        pl.semaphore_signal(barrier, 1, device_id={"work": peer(d)}, device_id_type=MESH)

    each(n_work - 1, greet)
    for other in (up, down):
        pl.semaphore_signal(barrier, 1, device_id={"slab": other}, device_id_type=MESH)

    lane = lax.broadcasted_iota(jnp.int32, (1, slots), 1)

    def filled_of(g):
        return (lane < counts[g]).astype(F32)

    for read in reads:
        read.wait()
    for g in range(nb):
        state = particles[:, g, :]
        near[mine + g] = jnp.concatenate([state[0:3], state[7:8] * filled_of(g)], axis=0)
        rest[mine + g] = state[3:7]

    pl.semaphore_wait(barrier, n_work + 1)

    def send(buf, step, slab_step):
        src = buf.at[pl.ds(mine, nb)]

        def start(dst, where, arrived):
            pltpu.make_async_remote_copy(
                src_ref=src,
                dst_ref=dst,
                send_sem=send_sem.at[step],
                recv_sem=recv_sem.at[arrived],
                device_id=where,
                device_id_type=MESH,
            ).start()

        start(buf.at[pl.ds(slab_bins, nb)], {"slab": up}, slab_step)
        start(buf.at[pl.ds(slab_bins + nb, nb)], {"slab": down}, slab_step)
        each(n_work - 1, lambda d: start(src, {"work": peer(d)}, step))

    def wait(buf, bins, sem):
        block = buf.at[pl.ds(0, bins)]
        pltpu.make_async_copy(block, block, sem).wait()

    everyone = slab_bins + nb
    send(near, 0, 3)

    def member_index(g, k):
        if k == 0:
            return mine + g
        if k == 1:
            return slab_bins + g
        if k == 2:
            return slab_bins + nb + g
        return partners[g, k - 3]

    row4 = sub_iota(4, slots)
    row8 = sub_iota(8, slots)
    spare = jnp.zeros((8, slots), F32)

    def centre(g):
        return jnp.mean(particles[0:7, g, :], axis=1, keepdims=True)

    def offset(values, mid):
        shifted = jnp.where(row4 < 3, values - mid, 0.0)
        return shifted, jnp.sum(shifted * shifted, axis=0, keepdims=True)

    def build_right(g, k, mid_pos):
        shifted, length = offset(near[member_index(g, k)], mid_pos)
        other = jnp.where(row4 < 3, shifted, length)
        q0, q1, q2 = pieces(jnp.concatenate([other, other], axis=0))
        row = row8 % 4
        one0 = jnp.where(row < 3, q0, 1.0)
        right = jnp.concatenate(
            [
                jnp.where(row8 < 4, q0, q1),
                jnp.where(row8 < 4, q2, one0),
                jnp.where(row8 < 4, jnp.where(row < 3, q1, 1.0), one0),
                spare,
            ],
            axis=0,
        )
        right_ops[g, :, k * slots : (k + 1) * slots] = right.astype(BF16)

    centres = []
    for g in range(nb):
        mid = centre(g)
        mid_pos = jnp.concatenate([mid[0:3], jnp.zeros((1, 1), F32)], axis=0)
        centres.append((mid_pos, mid[3:6]))
        shifted, length = offset(near[mine + g], mid_pos)
        own = jnp.where(row4 < 3, -2.0 * shifted, length)
        p0, p1, p2 = pieces(jnp.concatenate([own, own], axis=0))
        row = row8 % 4
        a0 = jnp.where(row < 3, p0, 1.0)
        left = jnp.concatenate(
            [
                a0,
                jnp.where(row8 < 4, a0, jnp.where(row < 3, p1, p0)),
                jnp.where(row8 < 4, p1, p2),
                spare,
            ],
            axis=0,
        )
        left_ops[g] = left.T.astype(BF16)
        build_right(g, 0, mid_pos)
        h_row = particles[6, g : g + 1, :]
        h_wide[g] = jnp.broadcast_to(h_row, (slots, slots)).T
        reach[g] = 2.0 * h_wide[g]
        limit[g] = 2.5 * h_wide[g]

    def density_part(g, ks, acc):
        mid_pos = centres[g][0]
        for k in ks:
            if k:
                build_right(g, k, mid_pos)
        for k0 in range(ks[0], ks[-1] + 1, 2):
            pair = [k for k in (k0, k0 + 1) if k in ks]
            cols = slice(k0 * slots, (k0 + len(pair)) * slots)
            square = jnp.dot(left_ops[g], right_ops[g, :, cols], preferred_element_type=F32)
            square = jnp.maximum(square, 1e-30)
            dist = square * lax.rsqrt(square)
            radius[g, :, cols] = dist
            for k in pair:
                mass = near[member_index(g, k)][3:4]
                gap = jnp.maximum(
                    reach[g] - dist[:, (k - k0) * slots : (k - k0 + 1) * slots], 0.0
                )
                gap2 = gap * gap
                acc += (gap2 * gap2) * ((limit[g] - gap) * mass)
        return acc

    def force_part(g, ks):
        for k in ks:
            cols = slice(k * slots, (k + 1) * slots)
            both = h_wide[g] + rest[member_index(g, k)][3:4]
            inv = pltpu.reciprocal(both, approx=True)
            inv2 = inv * inv
            gap = jnp.maximum(both - radius[g, :, cols], 0.0)
            part = gap * inv2
            force = (part * part) * (part * inv2)
            high = force.astype(BF16)
            force_hi[g, :, cols] = high
            force_lo[g, :, cols] = (force - high.astype(F32)).astype(BF16)

    for g in range(nb):
        partial[g] = density_part(g, range(1), jnp.zeros((slots, slots), F32))
        force_part(g, range(1))
    wait(near, 2 * nb, recv_sem.at[3])
    for g in range(nb):
        partial[g] = density_part(g, range(1, 3), partial[g])
    wait(near, slab_bins - nb, recv_sem.at[0])
    send(rest, 1, 1)

    for g in range(nb):
        acc = density_part(g, range(3, members), partial[g])
        total = jnp.sum(acc.T, axis=0, keepdims=True)
        filled = filled_of(g)
        h_row = particles[6, g : g + 1, :]
        h2 = h_row * h_row
        raw = total * ((weight_norm / 8.0) / (h2 * h2 * h2 * h2))
        density_out[g : g + 1, :] = filled * raw
        invs[mine + g] = 1.0 / (filled * raw + (1.0 - filled))

    send(invs, 2, 2)
    wait(rest, everyone, recv_sem.at[1])

    for g in range(nb):
        force_part(g, range(1, members))

    for g in range(nb):
        mid_pos, mid_vel = centres[g]
        mid_four = jnp.concatenate([mid_vel, jnp.zeros((1, 1), F32)], axis=0)
        for k in range(members):
            at = member_index(g, k)
            place = near[at]
            mass = place[3:4]
            moment = jnp.where(row4 < 3, place - mid_pos, 1.0) * mass
            speed = jnp.where(row4 < 3, rest[at] - mid_four, 0.0) * mass
            cols = slice(k * slots, (k + 1) * slots)
            bases[g, 0:8, cols] = jnp.concatenate([moment, moment], axis=0)
            bases[g, 8:16, cols] = jnp.concatenate([speed, speed], axis=0)

    wait(invs, everyone, recv_sem.at[2])

    for g in range(nb):
        mid_pos, mid_vel = centres[g]
        for k in range(members):
            cols = slice(k * slots, (k + 1) * slots)
            inv = invs[member_index(g, k)]
            source = jnp.concatenate(
                [
                    bases[g, 0:8, cols] * jnp.where(row8 < 4, 1.0, inv),
                    bases[g, 8:16, cols] * inv,
                ],
                axis=0,
            )
            first = source.astype(BF16)
            sources[g, 0:16, cols] = first
            sources[g, 16:32, cols] = (source - first.astype(F32)).astype(BF16)
        dims = (((1,), (1,)), ((), ()))
        sums = lax.dot_general(
            force_hi[g], sources[g], dims, preferred_element_type=F32
        ) + lax.dot_general(force_lo[g], sources[g], dims, preferred_element_type=F32)
        sums = sums.T
        sums = sums[0:16] + sums[16:32]
        own = particles[:, g, :]
        pos = own[0:3] - mid_pos[0:3]
        vel = own[3:6] - mid_vel
        inv = invs[mine + g]
        s1, s0, t1, t0, tv = sums[0:3], sums[3:4], sums[4:7], sums[7:8], sums[8:11]
        result = inv * (pos * s0 - s1) + (pos * t0 - t1) - (viscosity * inv) * (vel * t0 - tv)
        accel_out[:, g, :] = result * (filled_of(g) * (32.0 * force_norm))

    for step, buf in enumerate((near, rest, invs)):
        wait(buf, everyone, send_sem.at[step])


def write_out(density, accel, density_out, accel_out, sem):
    copies = [
        pltpu.make_async_copy(src, dst, sem.at[i])
        for i, (src, dst) in enumerate(((density, density_out), (accel, accel_out)))
    ]
    for copy in copies:
        copy.start()
    for copy in copies:
        copy.wait()


def per_device(n_slab, n_work, particles, counts, partners):
    channels, nb, slots = particles.shape
    members = 3 + partners.shape[1]
    bins = (n_work + 2) * nb
    vmem = pl.BlockSpec(memory_space=pltpu.VMEM)
    hbm = pl.BlockSpec(memory_space=pltpu.HBM)
    pairs = nb * members * slots * slots
    results = (
        jax.ShapeDtypeStruct((nb, slots), F32),
        jax.ShapeDtypeStruct((3, nb, slots), F32),
    )
    computed = pl.pallas_call(
        functools.partial(kernel, n_slab, n_work),
        out_shape=results,
        in_specs=[hbm, hbm, hbm],
        out_specs=(vmem, vmem),
        scratch_shapes=[
            pltpu.VMEM(particles.shape, F32),
            pltpu.SMEM(counts.shape, counts.dtype),
            pltpu.SMEM(partners.shape, partners.dtype),
            pltpu.VMEM((bins, 4, slots), F32),
            pltpu.VMEM((bins, 4, slots), F32),
            pltpu.VMEM((bins, 1, slots), F32),
            pltpu.VMEM((nb, slots, 32), BF16),
            pltpu.VMEM((nb, slots, slots), F32),
            pltpu.VMEM((nb, slots, slots), F32),
            pltpu.VMEM((nb, slots, slots), F32),
            pltpu.VMEM((nb, 32, members * slots), BF16),
            pltpu.VMEM((nb, slots, members * slots), F32),
            pltpu.VMEM((nb, slots, members * slots), BF16),
            pltpu.VMEM((nb, slots, members * slots), BF16),
            pltpu.VMEM((nb, slots, slots), F32),
            pltpu.VMEM((nb, 16, members * slots), F32),
            pltpu.VMEM((nb, 32, members * slots), BF16),
            pltpu.SemaphoreType.DMA((3,)),
            pltpu.SemaphoreType.DMA((4,)),
            pltpu.SemaphoreType.DMA((3,)),
        ],
        compiler_params=pltpu.CompilerParams(
            collective_id=0, has_side_effects=True, vmem_limit_bytes=40 * 1024 * 1024
        ),
        cost_estimate=pl.CostEstimate(flops=40 * pairs, bytes_accessed=65536, transcendentals=0),
    )(*(pltpu.with_memory_space_constraint(a, pltpu.HBM) for a in (particles, counts, partners)))
    return pl.pallas_call(
        write_out,
        out_shape=results,
        in_specs=[vmem, vmem],
        out_specs=(hbm, hbm),
        scratch_shapes=[pltpu.SemaphoreType.DMA((2,))],
    )(*computed)


def solution(mesh):
    placed = (P(None, ("slab", "work"), None), P(("slab", "work")), P(("slab", "work"), None))
    return jax.shard_map(
        functools.partial(per_device, mesh.shape["slab"], mesh.shape["work"]),
        mesh=mesh,
        in_specs=placed,
        out_specs=(P(("slab", "work"), None), P(None, ("slab", "work"), None)),
        check_vma=False,
    )
```

```python
import functools

import jax
import jax.numpy as jnp
from jax import lax
from jax.experimental import pallas as pl
from jax.experimental.pallas import tpu as pltpu
from jax.sharding import PartitionSpec as P

weight_norm = 21.0 / (16.0 * 3.141592653589793)
force_norm = 105.0 / (16.0 * 3.141592653589793)
viscosity = 0.25

MESH = pl.DeviceIdType.MESH
F32 = jnp.float32
BF16 = jnp.bfloat16


def rounded(values):
    return values.astype(BF16).astype(F32)


def pieces(values):
    first = rounded(values)
    rest = values - first
    second = rounded(rest)
    return first, second, rest - second


def sub_iota(rows, slots):
    return lax.broadcasted_iota(jnp.int32, (rows, slots), 0)


def each(count, body):
    if count <= 16:
        for i in range(count):
            body(i)
    else:
        lax.fori_loop(0, count, lambda i, c: (body(i), c)[1], 0)


def kernel(
    n_slab,
    n_work,
    particles_in,
    counts_in,
    partners_in,
    density_out,
    accel_out,
    particles,
    counts,
    partners,
    near,
    rest,
    invs,
    left_ops,
    h_wide,
    reach,
    limit,
    right_ops,
    radius,
    force_hi,
    force_lo,
    partial,
    bases,
    sources,
    send_sem,
    recv_sem,
    read_sem,
):
    nb, slots = particles.shape[1], particles.shape[2]
    links = partners.shape[1]
    members = 3 + links
    slab = lax.axis_index("slab")
    me = lax.axis_index("work")
    mine = me * nb
    slab_bins = n_work * nb
    up = lax.rem(slab + 1, n_slab)
    down = lax.rem(slab + n_slab - 1, n_slab)

    reads = [
        pltpu.make_async_copy(src, dst, read_sem.at[i])
        for i, (src, dst) in enumerate(
            ((particles_in, particles), (counts_in, counts), (partners_in, partners))
        )
    ]
    for read in reads:
        read.start()

    barrier = pltpu.get_barrier_semaphore()

    def peer(d):
        if n_work & (n_work - 1):
            return lax.rem(me + d + 1, n_work)
        flips, other, bit = n_work - 1 - d, me, 1
        while bit < n_work:
            other = other + bit * ((flips // bit) % 2) * (1 - 2 * ((me // bit) % 2))
            bit *= 2
        return other

    def greet(d):
        pl.semaphore_signal(barrier, 1, device_id={"work": peer(d)}, device_id_type=MESH)

    each(n_work - 1, greet)
    for other in (up, down):
        pl.semaphore_signal(barrier, 1, device_id={"slab": other}, device_id_type=MESH)

    lane = lax.broadcasted_iota(jnp.int32, (1, slots), 1)

    def filled_of(g):
        return (lane < counts[g]).astype(F32)

    for read in reads:
        read.wait()
    for g in range(nb):
        state = particles[:, g, :]
        near[mine + g] = jnp.concatenate([state[0:3], state[7:8] * filled_of(g)], axis=0)
        rest[mine + g] = state[3:7]

    pl.semaphore_wait(barrier, n_work + 1)

    def send(buf, step, slab_step):
        src = buf.at[pl.ds(mine, nb)]

        def start(dst, where, arrived):
            pltpu.make_async_remote_copy(
                src_ref=src,
                dst_ref=dst,
                send_sem=send_sem.at[step],
                recv_sem=recv_sem.at[arrived],
                device_id=where,
                device_id_type=MESH,
            ).start()

        start(buf.at[pl.ds(slab_bins, nb)], {"slab": up}, slab_step)
        start(buf.at[pl.ds(slab_bins + nb, nb)], {"slab": down}, slab_step)
        each(n_work - 1, lambda d: start(src, {"work": peer(d)}, step))

    def wait(buf, bins, sem):
        block = buf.at[pl.ds(0, bins)]
        pltpu.make_async_copy(block, block, sem).wait()

    everyone = slab_bins + nb
    send(near, 0, 3)

    def member_index(g, k):
        if k == 0:
            return mine + g
        if k == 1:
            return slab_bins + g
        if k == 2:
            return slab_bins + nb + g
        return partners[g, k - 3]

    row4 = sub_iota(4, slots)
    row8 = sub_iota(8, slots)
    spare = jnp.zeros((8, slots), F32)

    def centre(g):
        return jnp.mean(particles[0:7, g, :], axis=1, keepdims=True)

    def offset(values, mid):
        shifted = jnp.where(row4 < 3, values - mid, 0.0)
        return shifted, jnp.sum(shifted * shifted, axis=0, keepdims=True)

    def build_right(g, k, mid_pos):
        shifted, length = offset(near[member_index(g, k)], mid_pos)
        other = jnp.where(row4 < 3, shifted, length)
        q0, q1, q2 = pieces(jnp.concatenate([other, other], axis=0))
        row = row8 % 4
        one0 = jnp.where(row < 3, q0, 1.0)
        right = jnp.concatenate(
            [
                jnp.where(row8 < 4, q0, q1),
                jnp.where(row8 < 4, q2, one0),
                jnp.where(row8 < 4, jnp.where(row < 3, q1, 1.0), one0),
                spare,
            ],
            axis=0,
        )
        right_ops[g, :, k * slots : (k + 1) * slots] = right.astype(BF16)

    centres = []
    for g in range(nb):
        mid = centre(g)
        mid_pos = jnp.concatenate([mid[0:3], jnp.zeros((1, 1), F32)], axis=0)
        centres.append((mid_pos, mid[3:6]))
        shifted, length = offset(near[mine + g], mid_pos)
        own = jnp.where(row4 < 3, -2.0 * shifted, length)
        p0, p1, p2 = pieces(jnp.concatenate([own, own], axis=0))
        row = row8 % 4
        a0 = jnp.where(row < 3, p0, 1.0)
        left = jnp.concatenate(
            [
                a0,
                jnp.where(row8 < 4, a0, jnp.where(row < 3, p1, p0)),
                jnp.where(row8 < 4, p1, p2),
                spare,
            ],
            axis=0,
        )
        left_ops[g] = left.T.astype(BF16)
        build_right(g, 0, mid_pos)
        h_row = particles[6, g : g + 1, :]
        h_wide[g] = jnp.broadcast_to(h_row, (slots, slots)).T
        reach[g] = 2.0 * h_wide[g]
        limit[g] = 2.5 * h_wide[g]

    def density_part(g, ks, acc):
        mid_pos = centres[g][0]
        for k in ks:
            if k:
                build_right(g, k, mid_pos)
        for k0 in range(ks[0], ks[-1] + 1, 2):
            pair = [k for k in (k0, k0 + 1) if k in ks]
            cols = slice(k0 * slots, (k0 + len(pair)) * slots)
            square = jnp.dot(left_ops[g], right_ops[g, :, cols], preferred_element_type=F32)
            square = jnp.maximum(square, 1e-30)
            dist = square * lax.rsqrt(square)
            radius[g, :, cols] = dist
            for k in pair:
                mass = near[member_index(g, k)][3:4]
                gap = jnp.maximum(
                    reach[g] - dist[:, (k - k0) * slots : (k - k0 + 1) * slots], 0.0
                )
                gap2 = gap * gap
                acc += (gap2 * gap2) * ((limit[g] - gap) * mass)
        return acc

    def force_part(g, ks):
        for k in ks:
            cols = slice(k * slots, (k + 1) * slots)
            both = h_wide[g] + rest[member_index(g, k)][3:4]
            inv = pltpu.reciprocal(both, approx=True)
            inv2 = inv * inv
            gap = jnp.maximum(both - radius[g, :, cols], 0.0)
            part = gap * inv2
            force = (part * part) * (part * inv2)
            high = force.astype(BF16)
            force_hi[g, :, cols] = high
            force_lo[g, :, cols] = (force - high.astype(F32)).astype(BF16)

    for g in range(nb):
        partial[g] = density_part(g, range(1), jnp.zeros((slots, slots), F32))
        force_part(g, range(1))
    wait(near, 2 * nb, recv_sem.at[3])
    for g in range(nb):
        partial[g] = density_part(g, range(1, 3), partial[g])
    wait(near, slab_bins - nb, recv_sem.at[0])
    send(rest, 1, 1)

    for g in range(nb):
        acc = density_part(g, range(3, members), partial[g])
        total = jnp.sum(acc.T, axis=0, keepdims=True)
        filled = filled_of(g)
        h_row = particles[6, g : g + 1, :]
        h2 = h_row * h_row
        raw = total * ((weight_norm / 8.0) / (h2 * h2 * h2 * h2))
        density_out[g : g + 1, :] = filled * raw
        invs[mine + g] = 1.0 / (filled * raw + (1.0 - filled))

    send(invs, 2, 2)
    wait(rest, everyone, recv_sem.at[1])

    for g in range(nb):
        force_part(g, range(1, members))

    for g in range(nb):
        mid_pos, mid_vel = centres[g]
        mid_four = jnp.concatenate([mid_vel, jnp.zeros((1, 1), F32)], axis=0)
        for k in range(members):
            at = member_index(g, k)
            place = near[at]
            mass = place[3:4]
            moment = jnp.where(row4 < 3, place - mid_pos, 1.0) * mass
            speed = jnp.where(row4 < 3, rest[at] - mid_four, 0.0) * mass
            cols = slice(k * slots, (k + 1) * slots)
            bases[g, 0:8, cols] = jnp.concatenate([moment, moment], axis=0)
            bases[g, 8:16, cols] = jnp.concatenate([speed, speed], axis=0)

    wait(invs, everyone, recv_sem.at[2])

    for g in range(nb):
        mid_pos, mid_vel = centres[g]
        for k in range(members):
            cols = slice(k * slots, (k + 1) * slots)
            inv = invs[member_index(g, k)]
            source = jnp.concatenate(
                [
                    bases[g, 0:8, cols] * jnp.where(row8 < 4, 1.0, inv),
                    bases[g, 8:16, cols] * inv,
                ],
                axis=0,
            )
            first = source.astype(BF16)
            sources[g, 0:16, cols] = first
            sources[g, 16:32, cols] = (source - first.astype(F32)).astype(BF16)
        dims = (((1,), (1,)), ((), ()))
        sums = lax.dot_general(
            force_hi[g], sources[g], dims, preferred_element_type=F32
        ) + lax.dot_general(force_lo[g], sources[g], dims, preferred_element_type=F32)
        sums = sums.T
        sums = sums[0:16] + sums[16:32]
        own = particles[:, g, :]
        pos = own[0:3] - mid_pos[0:3]
        vel = own[3:6] - mid_vel
        inv = invs[mine + g]
        s1, s0, t1, t0, tv = sums[0:3], sums[3:4], sums[4:7], sums[7:8], sums[8:11]
        result = inv * (pos * s0 - s1) + (pos * t0 - t1) - (viscosity * inv) * (vel * t0 - tv)
        accel_out[:, g, :] = result * (filled_of(g) * (32.0 * force_norm))

    for step, buf in enumerate((near, rest, invs)):
        wait(buf, everyone, send_sem.at[step])


def write_out(density, accel, density_out, accel_out, sem):
    copies = [
        pltpu.make_async_copy(src, dst, sem.at[i])
        for i, (src, dst) in enumerate(((density, density_out), (accel, accel_out)))
    ]
    for copy in copies:
        copy.start()
    for copy in copies:
        copy.wait()


def per_device(n_slab, n_work, particles, counts, partners):
    channels, nb, slots = particles.shape
    members = 3 + partners.shape[1]
    bins = (n_work + 2) * nb
    vmem = pl.BlockSpec(memory_space=pltpu.VMEM)
    hbm = pl.BlockSpec(memory_space=pltpu.HBM)
    pairs = nb * members * slots * slots
    results = (
        jax.ShapeDtypeStruct((nb, slots), F32),
        jax.ShapeDtypeStruct((3, nb, slots), F32),
    )
    computed = pl.pallas_call(
        functools.partial(kernel, n_slab, n_work),
        out_shape=results,
        in_specs=[hbm, hbm, hbm],
        out_specs=(vmem, vmem),
        scratch_shapes=[
            pltpu.VMEM(particles.shape, F32),
            pltpu.SMEM(counts.shape, counts.dtype),
            pltpu.SMEM(partners.shape, partners.dtype),
            pltpu.VMEM((bins, 4, slots), F32),
            pltpu.VMEM((bins, 4, slots), F32),
            pltpu.VMEM((bins, 1, slots), F32),
            pltpu.VMEM((nb, slots, 32), BF16),
            pltpu.VMEM((nb, slots, slots), F32),
            pltpu.VMEM((nb, slots, slots), F32),
            pltpu.VMEM((nb, slots, slots), F32),
            pltpu.VMEM((nb, 32, members * slots), BF16),
            pltpu.VMEM((nb, slots, members * slots), F32),
            pltpu.VMEM((nb, slots, members * slots), BF16),
            pltpu.VMEM((nb, slots, members * slots), BF16),
            pltpu.VMEM((nb, slots, slots), F32),
            pltpu.VMEM((nb, 16, members * slots), F32),
            pltpu.VMEM((nb, 32, members * slots), BF16),
            pltpu.SemaphoreType.DMA((3,)),
            pltpu.SemaphoreType.DMA((4,)),
            pltpu.SemaphoreType.DMA((3,)),
        ],
        compiler_params=pltpu.CompilerParams(
            collective_id=0, has_side_effects=True, vmem_limit_bytes=40 * 1024 * 1024
        ),
        cost_estimate=pl.CostEstimate(flops=40 * pairs, bytes_accessed=65536, transcendentals=0),
    )(*(pltpu.with_memory_space_constraint(a, pltpu.HBM) for a in (particles, counts, partners)))
    return pl.pallas_call(
        write_out,
        out_shape=results,
        in_specs=[vmem, vmem],
        out_specs=(hbm, hbm),
        scratch_shapes=[pltpu.SemaphoreType.DMA((2,))],
        compiler_params=pltpu.CompilerParams(vmem_limit_bytes=1024 * 1024),
    )(*(pltpu.with_memory_space_constraint(a, pltpu.VMEM) for a in computed))


def solution(mesh):
    placed = (P(None, ("slab", "work"), None), P(("slab", "work")), P(("slab", "work"), None))
    return jax.shard_map(
        functools.partial(per_device, mesh.shape["slab"], mesh.shape["work"]),
        mesh=mesh,
        in_specs=placed,
        out_specs=(P(("slab", "work"), None), P(None, ("slab", "work"), None)),
        check_vma=False,
    )
```

```python
import functools

import jax
import jax.numpy as jnp
from jax import lax
from jax.experimental import pallas as pl
from jax.experimental.pallas import tpu as pltpu
from jax.sharding import PartitionSpec as P

weight_norm = 21.0 / (16.0 * 3.141592653589793)
force_norm = 105.0 / (16.0 * 3.141592653589793)
viscosity = 0.25

MESH = pl.DeviceIdType.MESH
F32 = jnp.float32
BF16 = jnp.bfloat16


def rounded(values):
    return values.astype(BF16).astype(F32)


def pieces(values):
    first = rounded(values)
    rest = values - first
    second = rounded(rest)
    return first, second, rest - second


def sub_iota(rows, slots):
    return lax.broadcasted_iota(jnp.int32, (rows, slots), 0)


def each(count, body):
    if count <= 16:
        for i in range(count):
            body(i)
    else:
        lax.fori_loop(0, count, lambda i, c: (body(i), c)[1], 0)


def kernel(
    n_slab,
    n_work,
    particles_in,
    counts_in,
    partners_in,
    density_out,
    accel_out,
    particles,
    counts,
    partners,
    near,
    rest,
    invs,
    left_ops,
    h_wide,
    reach,
    limit,
    right_ops,
    radius,
    force_hi,
    force_lo,
    partial,
    bases,
    sources,
    send_sem,
    recv_sem,
    read_sem,
):
    nb, slots = particles.shape[1], particles.shape[2]
    links = partners.shape[1]
    members = 3 + links
    slab = lax.axis_index("slab")
    me = lax.axis_index("work")
    mine = me * nb
    slab_bins = n_work * nb
    up = lax.rem(slab + 1, n_slab)
    down = lax.rem(slab + n_slab - 1, n_slab)

    reads = [
        pltpu.make_async_copy(src, dst, read_sem.at[i])
        for i, (src, dst) in enumerate(
            ((particles_in, particles), (counts_in, counts), (partners_in, partners))
        )
    ]
    for read in reads:
        read.start()

    barrier = pltpu.get_barrier_semaphore()

    def peer(d):
        if n_work & (n_work - 1):
            return lax.rem(me + d + 1, n_work)
        flips, other, bit = n_work - 1 - d, me, 1
        while bit < n_work:
            other = other + bit * ((flips // bit) % 2) * (1 - 2 * ((me // bit) % 2))
            bit *= 2
        return other

    def greet(d):
        pl.semaphore_signal(barrier, 1, device_id={"work": peer(d)}, device_id_type=MESH)

    each(n_work - 1, greet)
    for other in (up, down):
        pl.semaphore_signal(barrier, 1, device_id={"slab": other}, device_id_type=MESH)

    lane = lax.broadcasted_iota(jnp.int32, (1, slots), 1)

    def filled_of(g):
        return (lane < counts[g]).astype(F32)

    for read in reads:
        read.wait()
    for g in range(nb):
        state = particles[:, g, :]
        near[mine + g] = jnp.concatenate([state[0:3], state[7:8] * filled_of(g)], axis=0)
        rest[mine + g] = state[3:7]

    pl.semaphore_wait(barrier, n_work + 1)

    def send(buf, step, slab_step):
        src = buf.at[pl.ds(mine, nb)]

        def start(dst, where, arrived):
            pltpu.make_async_remote_copy(
                src_ref=src,
                dst_ref=dst,
                send_sem=send_sem.at[step],
                recv_sem=recv_sem.at[arrived],
                device_id=where,
                device_id_type=MESH,
            ).start()

        start(buf.at[pl.ds(slab_bins, nb)], {"slab": up}, slab_step)
        start(buf.at[pl.ds(slab_bins + nb, nb)], {"slab": down}, slab_step)
        each(n_work - 1, lambda d: start(src, {"work": peer(d)}, step))

    def wait(buf, bins, sem):
        block = buf.at[pl.ds(0, bins)]
        pltpu.make_async_copy(block, block, sem).wait()

    everyone = slab_bins + nb
    send(near, 0, 3)

    def member_index(g, k):
        if k == 0:
            return mine + g
        if k == 1:
            return slab_bins + g
        if k == 2:
            return slab_bins + nb + g
        return partners[g, k - 3]

    row4 = sub_iota(4, slots)
    row8 = sub_iota(8, slots)
    spare = jnp.zeros((8, slots), F32)

    def centre(g):
        return jnp.mean(particles[0:7, g, :], axis=1, keepdims=True)

    def offset(values, mid):
        shifted = jnp.where(row4 < 3, values - mid, 0.0)
        return shifted, jnp.sum(shifted * shifted, axis=0, keepdims=True)

    def build_right(g, k, mid_pos):
        shifted, length = offset(near[member_index(g, k)], mid_pos)
        other = jnp.where(row4 < 3, shifted, length)
        q0, q1, q2 = pieces(jnp.concatenate([other, other], axis=0))
        row = row8 % 4
        one0 = jnp.where(row < 3, q0, 1.0)
        right = jnp.concatenate(
            [
                jnp.where(row8 < 4, q0, q1),
                jnp.where(row8 < 4, q2, one0),
                jnp.where(row8 < 4, jnp.where(row < 3, q1, 1.0), one0),
                spare,
            ],
            axis=0,
        )
        right_ops[g, :, k * slots : (k + 1) * slots] = right.astype(BF16)

    centres = []
    for g in range(nb):
        mid = centre(g)
        mid_pos = jnp.concatenate([mid[0:3], jnp.zeros((1, 1), F32)], axis=0)
        centres.append((mid_pos, mid[3:6]))
        shifted, length = offset(near[mine + g], mid_pos)
        own = jnp.where(row4 < 3, -2.0 * shifted, length)
        p0, p1, p2 = pieces(jnp.concatenate([own, own], axis=0))
        row = row8 % 4
        a0 = jnp.where(row < 3, p0, 1.0)
        left = jnp.concatenate(
            [
                a0,
                jnp.where(row8 < 4, a0, jnp.where(row < 3, p1, p0)),
                jnp.where(row8 < 4, p1, p2),
                spare,
            ],
            axis=0,
        )
        left_ops[g] = left.T.astype(BF16)
        build_right(g, 0, mid_pos)
        h_row = particles[6, g : g + 1, :]
        h_wide[g] = jnp.broadcast_to(h_row, (slots, slots)).T
        reach[g] = 2.0 * h_wide[g]
        limit[g] = 2.5 * h_wide[g]

    def density_part(g, ks, acc):
        mid_pos = centres[g][0]
        for k in ks:
            if k:
                build_right(g, k, mid_pos)
        for k0 in range(ks[0], ks[-1] + 1, 2):
            pair = [k for k in (k0, k0 + 1) if k in ks]
            cols = slice(k0 * slots, (k0 + len(pair)) * slots)
            square = jnp.dot(left_ops[g], right_ops[g, :, cols], preferred_element_type=F32)
            square = jnp.maximum(square, 1e-30)
            dist = square * lax.rsqrt(square)
            radius[g, :, cols] = dist
            for k in pair:
                mass = near[member_index(g, k)][3:4]
                gap = jnp.maximum(
                    reach[g] - dist[:, (k - k0) * slots : (k - k0 + 1) * slots], 0.0
                )
                gap2 = gap * gap
                acc += (gap2 * gap2) * ((limit[g] - gap) * mass)
        return acc

    def force_part(g, ks):
        for k in ks:
            cols = slice(k * slots, (k + 1) * slots)
            both = h_wide[g] + rest[member_index(g, k)][3:4]
            inv = pltpu.reciprocal(both, approx=True)
            inv2 = inv * inv
            gap = jnp.maximum(both - radius[g, :, cols], 0.0)
            part = gap * inv2
            force = (part * part) * (part * inv2)
            high = force.astype(BF16)
            force_hi[g, :, cols] = high
            force_lo[g, :, cols] = (force - high.astype(F32)).astype(BF16)

    for g in range(nb):
        partial[g] = density_part(g, range(1), jnp.zeros((slots, slots), F32))
        force_part(g, range(1))
    wait(near, 2 * nb, recv_sem.at[3])
    send(rest, 1, 1)
    for g in range(nb):
        partial[g] = density_part(g, range(1, 3), partial[g])
    wait(near, slab_bins - nb, recv_sem.at[0])

    for g in range(nb):
        acc = density_part(g, range(3, members), partial[g])
        total = jnp.sum(acc.T, axis=0, keepdims=True)
        filled = filled_of(g)
        h_row = particles[6, g : g + 1, :]
        h2 = h_row * h_row
        raw = total * ((weight_norm / 8.0) / (h2 * h2 * h2 * h2))
        density_out[g : g + 1, :] = filled * raw
        invs[mine + g] = 1.0 / (filled * raw + (1.0 - filled))

    send(invs, 2, 2)
    wait(rest, everyone, recv_sem.at[1])

    for g in range(nb):
        force_part(g, range(1, members))

    for g in range(nb):
        mid_pos, mid_vel = centres[g]
        mid_four = jnp.concatenate([mid_vel, jnp.zeros((1, 1), F32)], axis=0)
        for k in range(members):
            at = member_index(g, k)
            place = near[at]
            mass = place[3:4]
            moment = jnp.where(row4 < 3, place - mid_pos, 1.0) * mass
            speed = jnp.where(row4 < 3, rest[at] - mid_four, 0.0) * mass
            cols = slice(k * slots, (k + 1) * slots)
            bases[g, 0:8, cols] = jnp.concatenate([moment, moment], axis=0)
            bases[g, 8:16, cols] = jnp.concatenate([speed, speed], axis=0)

    wait(invs, everyone, recv_sem.at[2])

    for g in range(nb):
        mid_pos, mid_vel = centres[g]
        for k in range(members):
            cols = slice(k * slots, (k + 1) * slots)
            inv = invs[member_index(g, k)]
            source = jnp.concatenate(
                [
                    bases[g, 0:8, cols] * jnp.where(row8 < 4, 1.0, inv),
                    bases[g, 8:16, cols] * inv,
                ],
                axis=0,
            )
            first = source.astype(BF16)
            sources[g, 0:16, cols] = first
            sources[g, 16:32, cols] = (source - first.astype(F32)).astype(BF16)
        dims = (((1,), (1,)), ((), ()))
        sums = lax.dot_general(
            force_hi[g], sources[g], dims, preferred_element_type=F32
        ) + lax.dot_general(force_lo[g], sources[g], dims, preferred_element_type=F32)
        sums = sums.T
        sums = sums[0:16] + sums[16:32]
        own = particles[:, g, :]
        pos = own[0:3] - mid_pos[0:3]
        vel = own[3:6] - mid_vel
        inv = invs[mine + g]
        s1, s0, t1, t0, tv = sums[0:3], sums[3:4], sums[4:7], sums[7:8], sums[8:11]
        result = inv * (pos * s0 - s1) + (pos * t0 - t1) - (viscosity * inv) * (vel * t0 - tv)
        accel_out[:, g, :] = result * (filled_of(g) * (32.0 * force_norm))

    for step, buf in enumerate((near, rest, invs)):
        wait(buf, everyone, send_sem.at[step])


def write_out(density, accel, density_out, accel_out, sem):
    copies = [
        pltpu.make_async_copy(src, dst, sem.at[i])
        for i, (src, dst) in enumerate(((density, density_out), (accel, accel_out)))
    ]
    for copy in copies:
        copy.start()
    for copy in copies:
        copy.wait()


def per_device(n_slab, n_work, particles, counts, partners):
    channels, nb, slots = particles.shape
    members = 3 + partners.shape[1]
    bins = (n_work + 2) * nb
    vmem = pl.BlockSpec(memory_space=pltpu.VMEM)
    hbm = pl.BlockSpec(memory_space=pltpu.HBM)
    pairs = nb * members * slots * slots
    results = (
        jax.ShapeDtypeStruct((nb, slots), F32),
        jax.ShapeDtypeStruct((3, nb, slots), F32),
    )
    computed = pl.pallas_call(
        functools.partial(kernel, n_slab, n_work),
        out_shape=results,
        in_specs=[hbm, hbm, hbm],
        out_specs=(vmem, vmem),
        scratch_shapes=[
            pltpu.VMEM(particles.shape, F32),
            pltpu.SMEM(counts.shape, counts.dtype),
            pltpu.SMEM(partners.shape, partners.dtype),
            pltpu.VMEM((bins, 4, slots), F32),
            pltpu.VMEM((bins, 4, slots), F32),
            pltpu.VMEM((bins, 1, slots), F32),
            pltpu.VMEM((nb, slots, 32), BF16),
            pltpu.VMEM((nb, slots, slots), F32),
            pltpu.VMEM((nb, slots, slots), F32),
            pltpu.VMEM((nb, slots, slots), F32),
            pltpu.VMEM((nb, 32, members * slots), BF16),
            pltpu.VMEM((nb, slots, members * slots), F32),
            pltpu.VMEM((nb, slots, members * slots), BF16),
            pltpu.VMEM((nb, slots, members * slots), BF16),
            pltpu.VMEM((nb, slots, slots), F32),
            pltpu.VMEM((nb, 16, members * slots), F32),
            pltpu.VMEM((nb, 32, members * slots), BF16),
            pltpu.SemaphoreType.DMA((3,)),
            pltpu.SemaphoreType.DMA((4,)),
            pltpu.SemaphoreType.DMA((3,)),
        ],
        compiler_params=pltpu.CompilerParams(
            collective_id=0, has_side_effects=True, vmem_limit_bytes=40 * 1024 * 1024
        ),
        cost_estimate=pl.CostEstimate(flops=40 * pairs, bytes_accessed=65536, transcendentals=0),
    )(*(pltpu.with_memory_space_constraint(a, pltpu.HBM) for a in (particles, counts, partners)))
    return pl.pallas_call(
        write_out,
        out_shape=results,
        in_specs=[vmem, vmem],
        out_specs=(hbm, hbm),
        scratch_shapes=[pltpu.SemaphoreType.DMA((2,))],
        compiler_params=pltpu.CompilerParams(vmem_limit_bytes=1024 * 1024),
    )(*(pltpu.with_memory_space_constraint(a, pltpu.VMEM) for a in computed))


def solution(mesh):
    placed = (P(None, ("slab", "work"), None), P(("slab", "work")), P(("slab", "work"), None))
    return jax.shard_map(
        functools.partial(per_device, mesh.shape["slab"], mesh.shape["work"]),
        mesh=mesh,
        in_specs=placed,
        out_specs=(P(("slab", "work"), None), P(None, ("slab", "work"), None)),
        check_vma=False,
    )
```

```python
import functools

import jax
import jax.numpy as jnp
from jax import lax
from jax.experimental import pallas as pl
from jax.experimental.pallas import tpu as pltpu
from jax.sharding import PartitionSpec as P

weight_norm = 21.0 / (16.0 * 3.141592653589793)
force_norm = 105.0 / (16.0 * 3.141592653589793)
viscosity = 0.25

MESH = pl.DeviceIdType.MESH
F32 = jnp.float32
BF16 = jnp.bfloat16


def rounded(values):
    return values.astype(BF16).astype(F32)


def pieces(values):
    first = rounded(values)
    rest = values - first
    second = rounded(rest)
    return first, second, rest - second


def sub_iota(rows, slots):
    return lax.broadcasted_iota(jnp.int32, (rows, slots), 0)


def each(count, body):
    if count <= 16:
        for i in range(count):
            body(i)
    else:
        lax.fori_loop(0, count, lambda i, c: (body(i), c)[1], 0)


def kernel(
    n_slab,
    n_work,
    particles_in,
    counts_in,
    partners_in,
    density_out,
    accel_out,
    particles,
    counts,
    partners,
    near,
    rest,
    invs,
    left_ops,
    h_wide,
    reach,
    limit,
    right_ops,
    radius,
    force_hi,
    force_lo,
    partial,
    bases,
    sources,
    send_sem,
    recv_sem,
    read_sem,
):
    nb, slots = particles.shape[1], particles.shape[2]
    links = partners.shape[1]
    members = 3 + links
    slab = lax.axis_index("slab")
    me = lax.axis_index("work")
    mine = me * nb
    slab_bins = n_work * nb
    up = lax.rem(slab + 1, n_slab)
    down = lax.rem(slab + n_slab - 1, n_slab)

    reads = [
        pltpu.make_async_copy(src, dst, read_sem.at[i])
        for i, (src, dst) in enumerate(
            ((particles_in, particles), (counts_in, counts), (partners_in, partners))
        )
    ]
    for read in reads:
        read.start()

    barrier = pltpu.get_barrier_semaphore()

    def peer(d):
        if n_work & (n_work - 1):
            return lax.rem(me + d + 1, n_work)
        flips, other, bit = n_work - 1 - d, me, 1
        while bit < n_work:
            other = other + bit * ((flips // bit) % 2) * (1 - 2 * ((me // bit) % 2))
            bit *= 2
        return other

    def greet(d):
        pl.semaphore_signal(barrier, 1, device_id={"work": peer(d)}, device_id_type=MESH)

    each(n_work - 1, greet)
    for other in (up, down):
        pl.semaphore_signal(barrier, 1, device_id={"slab": other}, device_id_type=MESH)

    lane = lax.broadcasted_iota(jnp.int32, (1, slots), 1)

    def filled_of(g):
        return (lane < counts[g]).astype(F32)

    for read in reads:
        read.wait()
    for g in range(nb):
        state = particles[:, g, :]
        near[mine + g] = jnp.concatenate([state[0:3], state[7:8] * filled_of(g)], axis=0)
        rest[mine + g] = state[3:7]

    pl.semaphore_wait(barrier, n_work + 1)

    def send(buf, step, slab_step):
        src = buf.at[pl.ds(mine, nb)]

        def start(dst, where, arrived):
            pltpu.make_async_remote_copy(
                src_ref=src,
                dst_ref=dst,
                send_sem=send_sem.at[step],
                recv_sem=recv_sem.at[arrived],
                device_id=where,
                device_id_type=MESH,
            ).start()

        start(buf.at[pl.ds(slab_bins, nb)], {"slab": up}, slab_step)
        start(buf.at[pl.ds(slab_bins + nb, nb)], {"slab": down}, slab_step)
        each(n_work - 1, lambda d: start(src, {"work": peer(d)}, step))

    def wait(buf, bins, sem):
        block = buf.at[pl.ds(0, bins)]
        pltpu.make_async_copy(block, block, sem).wait()

    everyone = slab_bins + nb
    send(near, 0, 3)

    def member_index(g, k):
        if k == 0:
            return mine + g
        if k == 1:
            return slab_bins + g
        if k == 2:
            return slab_bins + nb + g
        return partners[g, k - 3]

    row4 = sub_iota(4, slots)
    row8 = sub_iota(8, slots)
    spare = jnp.zeros((8, slots), F32)

    def centre(g):
        return jnp.mean(particles[0:7, g, :], axis=1, keepdims=True)

    def offset(values, mid):
        shifted = jnp.where(row4 < 3, values - mid, 0.0)
        return shifted, jnp.sum(shifted * shifted, axis=0, keepdims=True)

    def build_right(g, k, mid_pos):
        shifted, length = offset(near[member_index(g, k)], mid_pos)
        other = jnp.where(row4 < 3, shifted, length)
        q0, q1, q2 = pieces(jnp.concatenate([other, other], axis=0))
        row = row8 % 4
        one0 = jnp.where(row < 3, q0, 1.0)
        right = jnp.concatenate(
            [
                jnp.where(row8 < 4, q0, q1),
                jnp.where(row8 < 4, q2, one0),
                jnp.where(row8 < 4, jnp.where(row < 3, q1, 1.0), one0),
                spare,
            ],
            axis=0,
        )
        right_ops[g, :, k * slots : (k + 1) * slots] = right.astype(BF16)

    centres = []
    for g in range(nb):
        mid = centre(g)
        mid_pos = jnp.concatenate([mid[0:3], jnp.zeros((1, 1), F32)], axis=0)
        centres.append((mid_pos, mid[3:6]))
        shifted, length = offset(near[mine + g], mid_pos)
        own = jnp.where(row4 < 3, -2.0 * shifted, length)
        p0, p1, p2 = pieces(jnp.concatenate([own, own], axis=0))
        row = row8 % 4
        a0 = jnp.where(row < 3, p0, 1.0)
        left = jnp.concatenate(
            [
                a0,
                jnp.where(row8 < 4, a0, jnp.where(row < 3, p1, p0)),
                jnp.where(row8 < 4, p1, p2),
                spare,
            ],
            axis=0,
        )
        left_ops[g] = left.T.astype(BF16)
        build_right(g, 0, mid_pos)
        h_row = particles[6, g : g + 1, :]
        h_wide[g] = jnp.broadcast_to(h_row, (slots, slots)).T
        reach[g] = 2.0 * h_wide[g]
        limit[g] = 2.5 * h_wide[g]

    def density_part(g, ks, acc):
        mid_pos = centres[g][0]
        for k in ks:
            if k:
                build_right(g, k, mid_pos)
        for k0 in range(ks[0], ks[-1] + 1, 2):
            pair = [k for k in (k0, k0 + 1) if k in ks]
            cols = slice(k0 * slots, (k0 + len(pair)) * slots)
            square = jnp.dot(left_ops[g], right_ops[g, :, cols], preferred_element_type=F32)
            square = jnp.maximum(square, 1e-30)
            dist = square * lax.rsqrt(square)
            radius[g, :, cols] = dist
            for k in pair:
                mass = near[member_index(g, k)][3:4]
                gap = jnp.maximum(
                    reach[g] - dist[:, (k - k0) * slots : (k - k0 + 1) * slots], 0.0
                )
                gap2 = gap * gap
                acc += (gap2 * gap2) * ((limit[g] - gap) * mass)
        return acc

    def force_part(g, ks):
        for k in ks:
            cols = slice(k * slots, (k + 1) * slots)
            both = h_wide[g] + rest[member_index(g, k)][3:4]
            inv = pltpu.reciprocal(both, approx=True)
            inv2 = inv * inv
            gap = jnp.maximum(both - radius[g, :, cols], 0.0)
            part = gap * inv2
            force = (part * part) * (part * inv2)
            high = force.astype(BF16)
            force_hi[g, :, cols] = high
            force_lo[g, :, cols] = (force - high.astype(F32)).astype(BF16)

    for g in range(nb):
        partial[g] = density_part(g, range(1), jnp.zeros((slots, slots), F32))
        force_part(g, range(1))
    wait(near, 2 * nb, recv_sem.at[3])
    send(rest, 1, 1)
    for g in range(nb):
        partial[g] = density_part(g, range(1, 3), partial[g])
    wait(near, slab_bins - nb, recv_sem.at[0])

    for g in range(nb):
        acc = density_part(g, range(3, members), partial[g])
        total = jnp.sum(acc.T, axis=0, keepdims=True)
        filled = filled_of(g)
        h_row = particles[6, g : g + 1, :]
        h2 = h_row * h_row
        raw = total * ((weight_norm / 8.0) / (h2 * h2 * h2 * h2))
        density_out[g : g + 1, :] = filled * raw
        invs[mine + g] = 1.0 / (filled * raw + (1.0 - filled))

    send(invs, 2, 4)
    wait(rest, everyone, recv_sem.at[1])

    for g in range(nb):
        force_part(g, range(1, members))

    for g in range(nb):
        mid_pos, mid_vel = centres[g]
        mid_four = jnp.concatenate([mid_vel, jnp.zeros((1, 1), F32)], axis=0)
        for k in range(members):
            at = member_index(g, k)
            place = near[at]
            mass = place[3:4]
            moment = jnp.where(row4 < 3, place - mid_pos, 1.0) * mass
            speed = jnp.where(row4 < 3, rest[at] - mid_four, 0.0) * mass
            cols = slice(k * slots, (k + 1) * slots)
            bases[g, 0:8, cols] = jnp.concatenate([moment, moment], axis=0)
            bases[g, 8:16, cols] = jnp.concatenate([speed, speed], axis=0)

    def source_part(g, ks):
        for k in ks:
            cols = slice(k * slots, (k + 1) * slots)
            inv = invs[member_index(g, k)]
            source = jnp.concatenate(
                [
                    bases[g, 0:8, cols] * jnp.where(row8 < 4, 1.0, inv),
                    bases[g, 8:16, cols] * inv,
                ],
                axis=0,
            )
            first = source.astype(BF16)
            sources[g, 0:16, cols] = first
            sources[g, 16:32, cols] = (source - first.astype(F32)).astype(BF16)

    for g in range(nb):
        source_part(g, range(1))
    wait(invs, 2 * nb, recv_sem.at[4])
    for g in range(nb):
        source_part(g, range(1, 3))
    wait(invs, slab_bins - nb, recv_sem.at[2])

    for g in range(nb):
        mid_pos, mid_vel = centres[g]
        source_part(g, range(3, members))
        dims = (((1,), (1,)), ((), ()))
        sums = lax.dot_general(
            force_hi[g], sources[g], dims, preferred_element_type=F32
        ) + lax.dot_general(force_lo[g], sources[g], dims, preferred_element_type=F32)
        sums = sums.T
        sums = sums[0:16] + sums[16:32]
        own = particles[:, g, :]
        pos = own[0:3] - mid_pos[0:3]
        vel = own[3:6] - mid_vel
        inv = invs[mine + g]
        s1, s0, t1, t0, tv = sums[0:3], sums[3:4], sums[4:7], sums[7:8], sums[8:11]
        result = inv * (pos * s0 - s1) + (pos * t0 - t1) - (viscosity * inv) * (vel * t0 - tv)
        accel_out[:, g, :] = result * (filled_of(g) * (32.0 * force_norm))

    for step, buf in enumerate((near, rest, invs)):
        wait(buf, everyone, send_sem.at[step])


def write_out(density, accel, density_out, accel_out, sem):
    copies = [
        pltpu.make_async_copy(src, dst, sem.at[i])
        for i, (src, dst) in enumerate(((density, density_out), (accel, accel_out)))
    ]
    for copy in copies:
        copy.start()
    for copy in copies:
        copy.wait()


def per_device(n_slab, n_work, particles, counts, partners):
    channels, nb, slots = particles.shape
    members = 3 + partners.shape[1]
    bins = (n_work + 2) * nb
    vmem = pl.BlockSpec(memory_space=pltpu.VMEM)
    hbm = pl.BlockSpec(memory_space=pltpu.HBM)
    pairs = nb * members * slots * slots
    results = (
        jax.ShapeDtypeStruct((nb, slots), F32),
        jax.ShapeDtypeStruct((3, nb, slots), F32),
    )
    computed = pl.pallas_call(
        functools.partial(kernel, n_slab, n_work),
        out_shape=results,
        in_specs=[hbm, hbm, hbm],
        out_specs=(vmem, vmem),
        scratch_shapes=[
            pltpu.VMEM(particles.shape, F32),
            pltpu.SMEM(counts.shape, counts.dtype),
            pltpu.SMEM(partners.shape, partners.dtype),
            pltpu.VMEM((bins, 4, slots), F32),
            pltpu.VMEM((bins, 4, slots), F32),
            pltpu.VMEM((bins, 1, slots), F32),
            pltpu.VMEM((nb, slots, 32), BF16),
            pltpu.VMEM((nb, slots, slots), F32),
            pltpu.VMEM((nb, slots, slots), F32),
            pltpu.VMEM((nb, slots, slots), F32),
            pltpu.VMEM((nb, 32, members * slots), BF16),
            pltpu.VMEM((nb, slots, members * slots), F32),
            pltpu.VMEM((nb, slots, members * slots), BF16),
            pltpu.VMEM((nb, slots, members * slots), BF16),
            pltpu.VMEM((nb, slots, slots), F32),
            pltpu.VMEM((nb, 16, members * slots), F32),
            pltpu.VMEM((nb, 32, members * slots), BF16),
            pltpu.SemaphoreType.DMA((3,)),
            pltpu.SemaphoreType.DMA((5,)),
            pltpu.SemaphoreType.DMA((3,)),
        ],
        compiler_params=pltpu.CompilerParams(
            collective_id=0, has_side_effects=True, vmem_limit_bytes=40 * 1024 * 1024
        ),
        cost_estimate=pl.CostEstimate(flops=40 * pairs, bytes_accessed=65536, transcendentals=0),
    )(*(pltpu.with_memory_space_constraint(a, pltpu.HBM) for a in (particles, counts, partners)))
    return pl.pallas_call(
        write_out,
        out_shape=results,
        in_specs=[vmem, vmem],
        out_specs=(hbm, hbm),
        scratch_shapes=[pltpu.SemaphoreType.DMA((2,))],
        compiler_params=pltpu.CompilerParams(vmem_limit_bytes=1024 * 1024),
    )(*(pltpu.with_memory_space_constraint(a, pltpu.VMEM) for a in computed))


def solution(mesh):
    placed = (P(None, ("slab", "work"), None), P(("slab", "work")), P(("slab", "work"), None))
    return jax.shard_map(
        functools.partial(per_device, mesh.shape["slab"], mesh.shape["work"]),
        mesh=mesh,
        in_specs=placed,
        out_specs=(P(("slab", "work"), None), P(None, ("slab", "work"), None)),
        check_vma=False,
    )
```
